32 devices in a mesh: tm: 8 (over y, x, core), cell: 4 (over z).
Axes of the slice: x: 2, y: 2, z: 4, core: 2. Of those that a mesh axis runs over, the one named last changes fastest.
Arguments:
- start_states: float32 [8, 3, 128, 512], P('tm', None, None, 'cell'), may hold values from -6 to 6
- ocean_mask: int32 [128, 512], P(None, 'cell'), may hold values 0 or 1
- depth_class: int32 [128, 512], P(None, 'cell'), may hold values from 0 to 7
- class_depth: float32 [8], replicated, may hold values from 0.2 to 1
- drag_rate: float32 [128, 512], P(None, 'cell'), may hold values from 0.02 to 0.3
- tide_cos: float32 [128, 512], P(None, 'cell'), may hold values from -3 to 3
- tide_sin: float32 [128, 512], P(None, 'cell'), may hold values from -3 to 3
Outputs:
- defect: float32 [8, 3, 128, 512], P('tm', None, None, 'cell')
- state_grad: float32 [8, 3, 128, 512], P('tm', None, None, 'cell')
- drag_grad: float32 [128, 512], P('tm', 'cell')
The draws below stay inside these ranges and needn't reach their ends.
All inputs are finite; a program needn't handle non-finite values. No bound on the sum of `ocean_mask` on one device may be relied on, other than what follows from the above.
Results may differ from the reference program's by a relative error of at most 0.00002.
Values sent between devices are 32-bit elements; how exact they have to be, the bound alone decides.
A program may use at most 64 MiB of HBM per device.

```python
import math
import jax
import jax.numpy as jnp
from jax import lax

LAT = 128
STEPS = 8
NCLASS = 8
LON = 512
SLICES = 8


def touch_ends(entries, own_key, low, largest):
    longest = entries.shape.index(max(entries.shape))
    spots = []
    for shift in (0, 1):
        where = [jax.random.randint(jax.random.fold_in(own_key, axis), (), 0, length) for axis, length in enumerate(entries.shape)]
        where[longest] = (where[longest] + shift) % entries.shape[longest]
        spots.append(tuple(where))
    return entries.at[spots[0]].set(low).at[spots[1]].set(largest)


def strengthened(array, rng, source, target, shards_of, factor):
    owner, partner = [(jnp.arange(array.shape[axis_at]) // (array.shape[axis_at] // shards_of)).reshape([-1 if axis == axis_at else 1 for axis in range(array.ndim)]) for axis_at in (source, target)]
    chosen = jax.random.permutation(rng, shards_of)[partner]
    strong = (owner == chosen) | (owner == (partner + shards_of // 2) % shards_of)
    return jnp.where(strong, factor * array, array)


def block_scale(key, dims, pieces, least, high):
    gain, own = 1.0, jax.random.fold_in(key, 6)
    for dim, parts in pieces:
        draws = jnp.exp(jax.random.uniform(jax.random.fold_in(own, dim), (parts,), jnp.float32, least / len(pieces), high / len(pieces)))
        gain = gain * jnp.repeat(draws, dims[dim] // parts).reshape([-1 if axis == dim else 1 for axis in range(len(dims))])
    return gain


def noise(own_key, extent, scale, most, pieces=(), kind=jnp.bfloat16):
    result = jax.random.normal(own_key, extent, jnp.float32) * scale
    if len(pieces) > 0:
        result = block_scale(own_key, extent, pieces, -0.22, 0.18) * result
    return jnp.clip(result, min=-most, max=most).astype(kind)


def noise_with(key, shape, scale, most, cuts, heavy, kind=jnp.bfloat16):
    result = scale * jax.random.normal(key, shape, jnp.float32)
    if cuts:
        result = result * block_scale(key, shape, cuts, -0.22, 0.18)
    return jnp.clip(strengthened(result, jax.random.fold_in(key, 3), *heavy), -most, most).astype(kind)


def setup_inputs(seed: int = 0) -> dict:
    key_list = jax.random.split(jax.random.key(seed), 8)
    return {
        "start_states": noise_with(key_list[0], (SLICES, 3, LAT, LON), 1.0, 6.0, ((0, 8), (3, 4)), (0, 2, 8, 2.0), jnp.float32),
        "ocean_mask": touch_ends((jax.random.randint(key_list[1], (LAT, LON), 0, 4) < 3).astype(jnp.int32), jax.random.fold_in(key_list[1], 1), 0, 1),
        "depth_class": touch_ends(jax.random.randint(key_list[2], (LAT, LON), 0, NCLASS), jax.random.fold_in(key_list[2], 1), 0, NCLASS - 1).astype(jnp.int32),
        "class_depth": jnp.clip(jax.random.uniform(key_list[3], (NCLASS,), jnp.float32, 0.2, 1.0), 0.2, 1.0),
        "drag_rate": jnp.clip(jnp.exp(math.log(0.3) - 2.7080503 * jax.random.uniform(key_list[4], (LAT, LON), jnp.float32) ** block_scale(key_list[4], (LAT, LON), ((1, 4),), -0.2, 0.2)), 0.02, 0.3),
        "tide_cos": noise(key_list[5], (LAT, LON), 0.5, 3.0, ((1, 4),), jnp.float32),
        "tide_sin": noise(key_list[6], (LAT, LON), 0.5, 3.0, ((1, 4),), jnp.float32),
    }


FLUX_RATE = 0.7
PRESS_RATE = 0.7
ROTATION_RATE = 0.15

def across_cols(values_in):
    return 0.5 * (jnp.roll(values_in, -1, axis=-1) - jnp.roll(values_in, 1, axis=-1))

def across_rows(values_in):
    zeros_row = jnp.zeros_like(values_in[..., :1, :])
    upper_rows = jnp.concatenate([values_in[..., 1:, :], zeros_row], axis=-2)
    lower_rows = jnp.concatenate([zeros_row, values_in[..., :-1, :]], axis=-2)
    return 0.5 * (upper_rows - lower_rows)

def coriolis(rows_count):
    latitude = math.pi * ((jnp.arange(rows_count, dtype=jnp.float32) + 0.5) / rows_count - 0.5)
    return (ROTATION_RATE * jnp.sin(latitude))[:, None]

def advance(current, sea_mask, depth_field, retain, forcing, rotation):
    spread = across_cols(depth_field * current[1]) + across_rows(depth_field * current[2])
    height = sea_mask * (current[0] - FLUX_RATE * spread)
    surface = height + forcing
    mask_keep = sea_mask * retain
    east_new = mask_keep * (current[1] - PRESS_RATE * across_cols(surface) + rotation * current[2])
    north_new = mask_keep * (current[2] - PRESS_RATE * across_rows(surface) - rotation * current[1])
    return jnp.stack([height, east_new, north_new])

def run_slice(initial, slice_index, sea_mask, depth_field, drag_rate, tide_cos, tide_sin):
    retain = 1.0 / (1.0 + drag_rate)
    rotation = coriolis(sea_mask.shape[0])
    current = initial * sea_mask
    phase_unit = 2.0 * math.pi / (SLICES * STEPS)
    for step_number in range(STEPS):
        phase_now = (slice_index * STEPS + step_number).astype(jnp.float32) * phase_unit
        forcing = jnp.cos(phase_now) * tide_cos + jnp.sin(phase_now) * tide_sin
        current = advance(current, sea_mask, depth_field, retain, forcing, rotation)
    return current

def reference(start_states, ocean_mask, depth_class, class_depth, drag_rate, tide_cos, tide_sin):
    sea_mask = ocean_mask.astype(jnp.float32)
    classes = jnp.arange(NCLASS, dtype=jnp.int32)
    depth_field = lax.optimization_barrier(jnp.sum(jnp.where(depth_class[..., None] == classes, class_depth, jnp.zeros_like(class_depth)), axis=-1))
    indices = jnp.arange(SLICES, dtype=jnp.int32)

    def forward(operands):
        initial, slice_index = operands
        return run_slice(initial, slice_index, sea_mask, depth_field, drag_rate, tide_cos, tide_sin)
    end_states = lax.map(forward, (start_states, indices))
    defect = sea_mask * (end_states - jnp.roll(start_states, -1, axis=0))

    def backward(operands):
        initial, slice_index, weight = operands

        def slice_map(start_in, drag_in):
            return run_slice(start_in, slice_index, sea_mask, depth_field, drag_in, tide_cos, tide_sin)
        _, pull_back = jax.vjp(slice_map, initial, drag_rate)
        return pull_back(weight)
    pulled, drag_terms = lax.map(backward, (start_states, indices, defect))
    state_grad = pulled - jnp.roll(defect, 1, axis=0)
    drag_grad = lax.optimization_barrier(jnp.sum(drag_terms, axis=0)) / SLICES
    return (defect, state_grad, drag_grad)
```

```python
import functools
import math

import jax
import jax.numpy as jnp
from jax import lax
from jax.experimental import pallas as pl
from jax.experimental.pallas import tpu as pltpu
from jax.sharding import PartitionSpec as P

STEPS = 8
FLUX_RATE = 0.7
PRESS_RATE = 0.7
ROTATION_RATE = 0.15

LANES = 128
RIM = 4 * STEPS
PAD = 8
BLOCK = 32
MESH = pl.DeviceIdType.MESH

SEA, KEEP, DEPTH, COS, SIN = range(5)


def kernel(
    slices,
    cells,
    start_ref,
    mask_ref,
    class_ref,
    table_ref,
    drag_ref,
    cos_ref,
    sin_ref,
    defect_out,
    grad_out,
    drag_out,
    start,
    mask,
    classes,
    drag,
    tides,
    statics,
    rotation,
    trig,
    height,
    east,
    north,
    east_rim,
    north_rim,
    flux,
    press,
    packed,
    arrived,
    next_rim,
    next_start,
    defect,
    behind,
    grad,
    total,
    shares,
    share_in,
    share_out,
    in_sem,
    out_sem,
    halo_send,
    halo_recv,
    next_send,
    next_recv,
    rim_send,
    rim_recv,
    behind_send,
    behind_recv,
    share_send,
    share_recv,
):
    rows = mask.shape[0]
    blocks = rows // BLOCK
    me = lax.axis_index("tm")
    cell = lax.axis_index("cell")
    ahead = lax.rem(me + 1, slices)
    back = lax.rem(me + slices - 1, slices)
    east_cell = lax.rem(cell + 1, cells)
    west_cell = lax.rem(cell + cells - 1, cells)

    barrier = pltpu.get_barrier_semaphore()
    for other in (west_cell, east_cell):
        pl.semaphore_signal(barrier, inc=1, device_id=(me, other), device_id_type=MESH)
    for step in range(1, slices):
        peer = lax.rem(me + step, slices)
        pl.semaphore_signal(barrier, inc=1, device_id=(peer, cell), device_id_type=MESH)

    loads = [
        pltpu.make_async_copy(source, target, in_sem.at[i])
        for i, (source, target) in enumerate(
            (
                (mask_ref, mask),
                (class_ref, classes),
                (drag_ref, drag),
                (cos_ref, tides.at[0]),
                (sin_ref, tides.at[1]),
                (start_ref.at[0], start),
            )
        )
    ]
    for load in loads:
        load.start()
    for load in loads:
        load.wait()

    lane = lax.broadcasted_iota(jnp.int32, (BLOCK, LANES), 1)
    first = lane == 0
    last = lane == LANES - 1
    slot = lane // RIM

    def span(b):
        return pl.ds(b * BLOCK, BLOCK)

    def across(body, rim):
        body_up = pltpu.roll(jnp.where(first, rim, body), LANES - 1, 1)
        body_down = pltpu.roll(jnp.where(last, rim, body), 1, 1)
        rim_up = pltpu.roll(jnp.where(first, body, rim), LANES - 1, 1)
        rim_down = pltpu.roll(jnp.where(last, body, rim), 1, 1)
        return (body_up - body_down, rim_up - rim_down)

    def across_body(body, rim):
        body_up = pltpu.roll(jnp.where(first, rim, body), LANES - 1, 1)
        body_down = pltpu.roll(jnp.where(last, rim, body), 1, 1)
        return body_up - body_down

    def along(ref, half, b):
        upper = ref[half, pl.ds(PAD + b * BLOCK + 1, BLOCK), :]
        lower = ref[half, pl.ds(PAD + b * BLOCK - 1, BLOCK), :]
        return upper - lower

    def inner(b):
        return pl.ds(PAD + b * BLOCK, BLOCK)

    def turned(value, by):
        return value if by == 0 else pltpu.roll(value, by * RIM, 1)

    def pack(parts):
        to_west = parts[0]
        to_east = parts[0]
        for f in range(1, 4):
            to_west = jnp.where(slot == f, parts[f], to_west)
            to_east = jnp.where(slot == (f + 3) % 4, parts[f], to_east)
        return to_west, to_east

    for b in range(blocks):
        at = span(b)
        sea = mask[at, :].astype(jnp.float32)
        depth = jnp.zeros((BLOCK, LANES), jnp.float32)
        kind = classes[at, :]
        for c in range(table_ref.shape[0]):
            depth = jnp.where(kind == c, table_ref[c], depth)
        depth = (0.5 * FLUX_RATE) * depth
        keep = sea / (1.0 + drag[at, :])
        cosine = (0.5 * PRESS_RATE) * tides[0, at, :]
        sine = (0.5 * PRESS_RATE) * tides[1, at, :]
        fields = (sea, keep, depth, cosine, sine)
        for f in range(5):
            statics[f, 0, at, :] = fields[f]
        west, east_side = pack([turned(fields[f + 1], f) for f in range(4)])
        packed[0, at, :] = west
        packed[1, at, :] = east_side
    for b in range(blocks - 1):
        parts = [turned(start[f, span(b), :], f) for f in range(3)]
        parts.append(turned(start[b, span(blocks - 1), :], 3))
        west, east_side = pack(parts)
        packed[0, pl.ds(rows + b * BLOCK, BLOCK), :] = west
        packed[1, pl.ds(rows + b * BLOCK, BLOCK), :] = east_side

    pl.semaphore_wait(barrier, slices + 1)

    halos = [
        pltpu.make_async_remote_copy(
            src_ref=packed.at[side],
            dst_ref=arrived.at[side],
            send_sem=halo_send.at[side],
            recv_sem=halo_recv.at[side],
            device_id=(me, other),
            device_id_type=MESH,
        )
        for side, other in ((0, west_cell), (1, east_cell))
    ]
    for halo in halos:
        halo.start()
    start_copy = pltpu.make_async_remote_copy(
        src_ref=start,
        dst_ref=next_start,
        send_sem=next_send,
        recv_sem=next_recv,
        device_id=(back, cell),
        device_id_type=MESH,
    )
    start_copy.start()

    latitude = lax.broadcasted_iota(jnp.int32, (rows, LANES), 0).astype(jnp.float32)
    latitude = math.pi * ((latitude + 0.5) / rows - 0.5)
    rotation[...] = ROTATION_RATE * jnp.sin(latitude)
    unit = 2.0 * math.pi / (slices * STEPS)
    number = lax.broadcasted_iota(jnp.int32, (STEPS, LANES), 0) + me * STEPS
    phase = number.astype(jnp.float32) * unit
    trig[0:STEPS, :] = jnp.cos(phase)
    trig[STEPS : 2 * STEPS, :] = jnp.sin(phase)
    blank = jnp.zeros((PAD, LANES), jnp.float32)
    for ref in (flux, press):
        for half in range(2):
            ref[half, 0:PAD, :] = blank
            ref[half, PAD + rows : 2 * PAD + rows, :] = blank
    for b in range(blocks):
        at = span(b)
        sea = statics[SEA, 0, at, :]
        height[0, at, :] = sea * start[0, at, :]
        east[0, at, :] = sea * start[1, at, :]
        north_now = sea * start[2, at, :]
        north[0, at, :] = north_now
        flux[0, inner(b), :] = statics[DEPTH, 0, at, :] * north_now

    for halo in halos:
        halo.wait_recv()
    relays = [
        pltpu.make_async_remote_copy(
            src_ref=arrived.at[side, pl.ds(rows, rows - BLOCK)],
            dst_ref=next_rim.at[side],
            send_sem=rim_send.at[side],
            recv_sem=rim_recv.at[side],
            device_id=(back, cell),
            device_id_type=MESH,
        )
        for side in range(2)
    ]
    for relay in relays:
        relay.start()

    def unpack(ref, at, f):
        both = jnp.where(
            slot == f, ref[0, at, :], jnp.where(slot == (f + 3) % 4, ref[1, at, :], 0.0)
        )
        return turned(both, (4 - f) % 4)

    def unpack_state(ref, offset, f, b):
        if b < blocks - 1:
            return unpack(ref, pl.ds(offset + b * BLOCK, BLOCK), f)
        return unpack(ref, pl.ds(offset + f * BLOCK, BLOCK), 3)

    for b in range(blocks):
        at = span(b)
        fields = [unpack(arrived, at, f) for f in range(4)]
        sea = jnp.where(fields[0] > 0.0, 1.0, 0.0)
        statics[SEA, 1, at, :] = sea
        for f in range(4):
            statics[f + 1, 1, at, :] = fields[f]
        state = [sea * unpack_state(arrived, rows, f, b) for f in range(3)]
        height[1, at, :] = state[0]
        east_rim[at, :] = state[1]
        north_rim[at, :] = state[2]
        flux[1, inner(b), :] = fields[1] * state[2]

    def forward(n, carry):
        cosine = trig[pl.ds(n, 1), :]
        sine = trig[pl.ds(STEPS + n, 1), :]
        for b in range(blocks):
            at = span(b)
            spread = across(
                statics[DEPTH, 0, at, :] * east[n, at, :],
                statics[DEPTH, 1, at, :] * east_rim[at, :],
            )
            for half in range(2):
                new = statics[SEA, half, at, :] * (
                    height[half, at, :] - (spread[half] + along(flux, half, b))
                )
                height[half, at, :] = new
                press[half, inner(b), :] = (0.5 * PRESS_RATE) * new + (
                    cosine * statics[COS, half, at, :] + sine * statics[SIN, half, at, :]
                )
        for b in range(blocks):
            at = span(b)
            slope = across(press[0, inner(b), :], press[1, inner(b), :])
            turn = rotation[at, :]
            for half in range(2):
                east_now = east[n, at, :] if half == 0 else east_rim[at, :]
                north_now = north[n, at, :] if half == 0 else north_rim[at, :]
                keep = statics[KEEP, half, at, :]
                east_new = keep * (east_now - slope[half] + turn * north_now)
                north_new = keep * (north_now - along(press, half, b) - turn * east_now)
                if half == 0:
                    east[n + 1, at, :] = east_new
                    north[n + 1, at, :] = north_new
                else:
                    east_rim[at, :] = east_new
                    north_rim[at, :] = north_new
                flux[half, inner(b), :] = statics[DEPTH, half, at, :] * north_new
        return carry

    lax.fori_loop(0, STEPS, forward, 0)

    start_copy.wait_recv()
    for b in range(blocks):
        at = span(b)
        sea = statics[SEA, 0, at, :]
        keep = statics[KEEP, 0, at, :]
        miss = sea * (height[0, at, :] - next_start[0, at, :])
        defect[0, at, :] = miss
        height[0, at, :] = miss
        end = east[STEPS, at, :]
        miss = sea * (end - next_start[1, at, :])
        defect[1, at, :] = miss
        east_part = keep * miss
        end_north = north[STEPS, at, :]
        miss = sea * (end_north - next_start[2, at, :])
        defect[2, at, :] = miss
        north_part = keep * miss
        total[at, :] = east_part * end + north_part * end_north
        grad[1, at, :] = east_part
        flux[0, inner(b), :] = north_part
    behind_copy = pltpu.make_async_remote_copy(
        src_ref=defect,
        dst_ref=behind,
        send_sem=behind_send,
        recv_sem=behind_recv,
        device_id=(ahead, cell),
        device_id_type=MESH,
    )
    behind_copy.start()
    defect_store = pltpu.make_async_copy(defect, defect_out.at[0], out_sem.at[0])
    defect_store.start()

    for relay in relays:
        relay.wait_recv()
    for b in range(blocks):
        at = span(b)
        sea = statics[SEA, 1, at, :]
        keep = statics[KEEP, 1, at, :]
        height[1, at, :] = sea * (height[1, at, :] - unpack_state(next_rim, 0, 0, b))
        east_rim[at, :] = keep * (east_rim[at, :] - unpack_state(next_rim, 0, 1, b))
        flux[1, inner(b), :] = keep * (north_rim[at, :] - unpack_state(next_rim, 0, 2, b))

    def adjoint_height(halves):
        for b in range(blocks):
            at = span(b)
            slope = across(grad[1, at, :], east_rim[at, :])
            for half in range(halves):
                new = statics[SEA, half, at, :] * (
                    height[half, at, :]
                    + (0.5 * PRESS_RATE) * (slope[half] + along(flux, half, b))
                )
                height[half, at, :] = new
                press[half, inner(b), :] = new

    def adjoint(i, carry):
        n = STEPS - 1 - i
        adjoint_height(2)
        for b in range(blocks):
            at = span(b)
            slope = across(press[0, inner(b), :], press[1, inner(b), :])
            turn = rotation[at, :]
            for half in range(2):
                east_part = grad[1, at, :] if half == 0 else east_rim[at, :]
                north_part = flux[half, inner(b), :]
                keep = statics[KEEP, half, at, :]
                depth = statics[DEPTH, half, at, :]
                east_new = keep * (east_part - turn * north_part + depth * slope[half])
                north_new = keep * (north_part + turn * east_part + depth * along(press, half, b))
                if half == 0:
                    grad[1, at, :] = east_new
                    total[at, :] = total[at, :] + (
                        east_new * east[n, at, :] + north_new * north[n, at, :]
                    )
                else:
                    east_rim[at, :] = east_new
                flux[half, inner(b), :] = north_new
        return carry

    lax.fori_loop(0, STEPS - 1, adjoint, 0)

    share = rows // slices
    for t in range(slices):
        shares[t] = total[t * share : (t + 1) * share, :]
    share_copies = []
    for step in range(1, slices):
        peer = lax.rem(me + step, slices)
        share_copies.append(
            pltpu.make_async_remote_copy(
                src_ref=shares.at[peer],
                dst_ref=share_in.at[step],
                send_sem=share_send.at[step],
                recv_sem=share_recv.at[step],
                device_id=(peer, cell),
                device_id_type=MESH,
            )
        )
    for copy in share_copies:
        copy.start()

    adjoint_height(2)
    behind_copy.wait_recv()
    for b in range(blocks):
        at = span(b)
        slope = across_body(press[0, inner(b), :], press[1, inner(b), :])
        turn = rotation[at, :]
        sea = statics[SEA, 0, at, :]
        depth = statics[DEPTH, 0, at, :]
        east_part = grad[1, at, :]
        north_part = flux[0, inner(b), :]
        grad[0, at, :] = height[0, at, :] - behind[0, at, :]
        grad[1, at, :] = (
            sea * (east_part - turn * north_part + depth * slope) - behind[1, at, :]
        )
        grad[2, at, :] = (
            sea * (north_part + turn * east_part + depth * along(press, 0, b))
            - behind[2, at, :]
        )
    grad_store = pltpu.make_async_copy(grad, grad_out.at[0], out_sem.at[1])
    grad_store.start()

    summed = shares[me]
    for step in range(1, slices):
        share_copies[step - 1].wait_recv()
        summed = summed + share_in[step]
    share_out[...] = summed * (-1.0 / slices)
    drag_store = pltpu.make_async_copy(share_out, drag_out, out_sem.at[2])
    drag_store.start()

    for copy in halos + [start_copy] + relays + [behind_copy] + share_copies:
        copy.wait_send()
    defect_store.wait()
    grad_store.wait()
    drag_store.wait()


def local(slices, cells, start_states, ocean_mask, depth_class, class_depth, drag_rate, tide_cos, tide_sin):
    rows, lanes = ocean_mask.shape
    assert lanes == LANES and rows == 4 * BLOCK and rows % slices == 0
    share = rows // slices

    def f32(*shape):
        return pltpu.VMEM(shape, jnp.float32)

    sems = pltpu.SemaphoreType.DMA
    hbm = pl.BlockSpec(memory_space=pl.ANY)
    wide = rows + 2 * PAD
    rim_rows = rows - BLOCK
    return pl.pallas_call(
        functools.partial(kernel, slices, cells),
        out_shape=(
            jax.ShapeDtypeStruct(start_states.shape, jnp.float32),
            jax.ShapeDtypeStruct(start_states.shape, jnp.float32),
            jax.ShapeDtypeStruct((share, lanes), jnp.float32),
        ),
        in_specs=[hbm, hbm, hbm, pl.BlockSpec(memory_space=pltpu.SMEM), hbm, hbm, hbm],
        out_specs=(hbm, hbm, hbm),
        scratch_shapes=[
            f32(3, rows, lanes),
            pltpu.VMEM((rows, lanes), jnp.int32),
            pltpu.VMEM((rows, lanes), jnp.int32),
            f32(rows, lanes),
            f32(2, rows, lanes),
            f32(5, 2, rows, lanes),
            f32(rows, lanes),
            f32(2 * STEPS, lanes),
            f32(2, rows, lanes),
            f32(STEPS + 1, rows, lanes),
            f32(STEPS + 1, rows, lanes),
            f32(rows, lanes),
            f32(rows, lanes),
            f32(2, wide, lanes),
            f32(2, wide, lanes),
            f32(2, rows + rim_rows, lanes),
            f32(2, rows + rim_rows, lanes),
            f32(2, rim_rows, lanes),
            f32(3, rows, lanes),
            f32(3, rows, lanes),
            f32(3, rows, lanes),
            f32(3, rows, lanes),
            f32(rows, lanes),
            f32(slices, share, lanes),
            f32(slices, share, lanes),
            f32(share, lanes),
            sems((6,)),
            sems((3,)),
            sems((2,)),
            sems((2,)),
            sems,
            sems,
            sems((2,)),
            sems((2,)),
            sems,
            sems,
            sems((slices,)),
            sems((slices,)),
        ],
        compiler_params=pltpu.CompilerParams(
            collective_id=0, has_side_effects=True, vmem_limit_bytes=32 * 1024 * 1024
        ),
    )(start_states, ocean_mask, depth_class, class_depth, drag_rate, tide_cos, tide_sin)


def solution(mesh):
    return jax.shard_map(
        functools.partial(local, mesh.shape["tm"], mesh.shape["cell"]),
        mesh=mesh,
        in_specs=(
            P("tm", None, None, "cell"),
            P(None, "cell"),
            P(None, "cell"),
            P(),
            P(None, "cell"),
            P(None, "cell"),
            P(None, "cell"),
        ),
        out_specs=(P("tm", None, None, "cell"), P("tm", None, None, "cell"), P("tm", "cell")),
        check_vma=False,
    )
```

```python
import functools
import math

import jax
import jax.numpy as jnp
from jax import lax
from jax.experimental import pallas as pl
from jax.experimental.pallas import tpu as pltpu
from jax.sharding import PartitionSpec as P

STEPS = 8
FLUX_RATE = 0.7
PRESS_RATE = 0.7
ROTATION_RATE = 0.15

LANES = 128
RIM = 4 * STEPS
PAD = 8
BLOCK = 32
MESH = pl.DeviceIdType.MESH

SEA, KEEP, DEPTH, COS, SIN = range(5)


def kernel(
    slices,
    cells,
    start_ref,
    mask_ref,
    class_ref,
    table_ref,
    drag_ref,
    cos_ref,
    sin_ref,
    defect_out,
    grad_out,
    drag_out,
    start,
    mask,
    classes,
    drag,
    tides,
    statics,
    rotation,
    trig,
    height,
    east,
    north,
    adjoint_east,
    flux,
    press,
    packed,
    arrived,
    next_rim,
    next_start,
    defect,
    behind,
    grad,
    total,
    shares,
    share_in,
    share_out,
    in_sem,
    out_sem,
    halo_send,
    halo_recv,
    next_send,
    next_recv,
    rim_send,
    rim_recv,
    behind_send,
    behind_recv,
    share_send,
    share_recv,
):
    rows = mask.shape[0]
    blocks = rows // BLOCK
    me = lax.axis_index("tm")
    cell = lax.axis_index("cell")
    ahead = lax.rem(me + 1, slices)
    back = lax.rem(me + slices - 1, slices)
    east_cell = lax.rem(cell + 1, cells)
    west_cell = lax.rem(cell + cells - 1, cells)

    barrier = pltpu.get_barrier_semaphore()
    for other in (west_cell, east_cell):
        pl.semaphore_signal(barrier, inc=1, device_id=(me, other), device_id_type=MESH)
    for step in range(1, slices):
        peer = lax.rem(me + step, slices)
        pl.semaphore_signal(barrier, inc=1, device_id=(peer, cell), device_id_type=MESH)

    loads = [
        pltpu.make_async_copy(source, target, in_sem.at[i])
        for i, (source, target) in enumerate(
            (
                (mask_ref, mask),
                (class_ref, classes),
                (drag_ref, drag),
                (cos_ref, tides.at[0]),
                (sin_ref, tides.at[1]),
                (start_ref.at[0], start),
            )
        )
    ]
    for load in loads:
        load.start()
    for load in loads:
        load.wait()

    lane = lax.broadcasted_iota(jnp.int32, (BLOCK, LANES), 1)
    slot = lane // RIM

    def span(b):
        return pl.ds(b * BLOCK, BLOCK)

    def across(value):
        return pltpu.roll(value, LANES - 1, 1) - pltpu.roll(value, 1, 1)

    def along(ref, half, b):
        upper = ref[half, pl.ds(PAD + b * BLOCK + 1, BLOCK), :]
        lower = ref[half, pl.ds(PAD + b * BLOCK - 1, BLOCK), :]
        return upper - lower

    def inner(b):
        return pl.ds(PAD + b * BLOCK, BLOCK)

    def turned(value, by):
        return value if by % 4 == 0 else pltpu.roll(value, by % 4 * RIM, 1)

    def pack(parts):
        west = parts[0]
        east_side = turned(parts[0], 2)
        for f in range(1, 4):
            west = jnp.where(slot == f, turned(parts[f], f), west)
            east_side = jnp.where(slot == (f + 1) % 4, turned(parts[f], f - 2), east_side)
        return west, east_side

    def own_edges(value):
        return jnp.where(slot == 3, value, turned(value, 2))

    for b in range(blocks):
        at = span(b)
        sea = mask[at, :].astype(jnp.float32)
        depth = jnp.zeros((BLOCK, LANES), jnp.float32)
        kind = classes[at, :]
        for c in range(table_ref.shape[0]):
            depth = jnp.where(kind == c, table_ref[c], depth)
        depth = (0.5 * FLUX_RATE) * depth
        keep = sea / (1.0 + drag[at, :])
        cosine = (0.5 * PRESS_RATE) * tides[0, at, :]
        sine = (0.5 * PRESS_RATE) * tides[1, at, :]
        fields = (sea, keep, depth, cosine, sine)
        for f in range(5):
            statics[f, 0, at, :] = fields[f]
        west, east_side = pack(fields[1:])
        packed[0, at, :] = west
        packed[1, at, :] = east_side
    for b in range(blocks - 1):
        parts = [start[f, span(b), :] for f in range(3)]
        parts.append(start[b, span(blocks - 1), :])
        west, east_side = pack(parts)
        packed[0, pl.ds(rows + b * BLOCK, BLOCK), :] = west
        packed[1, pl.ds(rows + b * BLOCK, BLOCK), :] = east_side

    pl.semaphore_wait(barrier, slices + 1)

    halos = [
        pltpu.make_async_remote_copy(
            src_ref=packed.at[side],
            dst_ref=arrived.at[side],
            send_sem=halo_send.at[side],
            recv_sem=halo_recv.at[side],
            device_id=(me, other),
            device_id_type=MESH,
        )
        for side, other in ((0, west_cell), (1, east_cell))
    ]
    for halo in halos:
        halo.start()
    start_copy = pltpu.make_async_remote_copy(
        src_ref=start,
        dst_ref=next_start,
        send_sem=next_send,
        recv_sem=next_recv,
        device_id=(back, cell),
        device_id_type=MESH,
    )
    start_copy.start()

    latitude = lax.broadcasted_iota(jnp.int32, (rows, LANES), 0).astype(jnp.float32)
    latitude = math.pi * ((latitude + 0.5) / rows - 0.5)
    rotation[...] = ROTATION_RATE * jnp.sin(latitude)
    unit = 2.0 * math.pi / (slices * STEPS)
    number = lax.broadcasted_iota(jnp.int32, (STEPS, LANES), 0) + me * STEPS
    phase = number.astype(jnp.float32) * unit
    trig[0:STEPS, :] = jnp.cos(phase)
    trig[STEPS : 2 * STEPS, :] = jnp.sin(phase)
    blank = jnp.zeros((PAD, LANES), jnp.float32)
    for ref in (flux, press):
        for half in range(2):
            ref[half, 0:PAD, :] = blank
            ref[half, PAD + rows : 2 * PAD + rows, :] = blank
    for b in range(blocks):
        at = span(b)
        sea = statics[SEA, 0, at, :]
        height[0, at, :] = sea * start[0, at, :]
        east[0, 0, at, :] = sea * start[1, at, :]
        north_now = sea * start[2, at, :]
        north[0, 0, at, :] = north_now
        flux[0, inner(b), :] = statics[DEPTH, 0, at, :] * north_now

    def forward(half, n, carry):
        cosine = trig[pl.ds(n, 1), :]
        sine = trig[pl.ds(STEPS + n, 1), :]
        for b in range(blocks):
            at = span(b)
            spread = across(statics[DEPTH, half, at, :] * east[n, half, at, :])
            new = statics[SEA, half, at, :] * (
                height[half, at, :] - (spread + along(flux, half, b))
            )
            height[half, at, :] = new
            press[half, inner(b), :] = (0.5 * PRESS_RATE) * new + (
                cosine * statics[COS, half, at, :] + sine * statics[SIN, half, at, :]
            )
        for b in range(blocks):
            at = span(b)
            turn = rotation[at, :]
            east_now = east[n, half, at, :]
            north_now = north[n, half, at, :]
            keep = statics[KEEP, half, at, :]
            north_new = keep * (north_now - along(press, half, b) - turn * east_now)
            east[n + 1, half, at, :] = keep * (
                east_now - across(press[half, inner(b), :]) + turn * north_now
            )
            north[n + 1, half, at, :] = north_new
            flux[half, inner(b), :] = statics[DEPTH, half, at, :] * north_new
        return carry

    lax.fori_loop(0, STEPS, functools.partial(forward, 0), 0)

    for halo in halos:
        halo.wait_recv()
    relays = [
        pltpu.make_async_remote_copy(
            src_ref=arrived.at[side, pl.ds(rows, rows - BLOCK)],
            dst_ref=next_rim.at[side],
            send_sem=rim_send.at[side],
            recv_sem=rim_recv.at[side],
            device_id=(back, cell),
            device_id_type=MESH,
        )
        for side in range(2)
    ]
    for relay in relays:
        relay.start()

    def unpack(ref, at, f, own):
        rims = turned(
            jnp.where(slot == f, ref[0, at, :], ref[1, at, :]),
            -f,
        )
        return jnp.where(slot < 2, rims, own_edges(own))

    def unpack_state(ref, offset, f, b, own):
        if b < blocks - 1:
            return unpack(ref, pl.ds(offset + b * BLOCK, BLOCK), f, own)
        return unpack(ref, pl.ds(offset + f * BLOCK, BLOCK), 3, own)

    for b in range(blocks):
        at = span(b)
        fields = [unpack(arrived, at, f, statics[f + 1, 0, at, :]) for f in range(4)]
        sea = jnp.where(fields[0] > 0.0, 1.0, 0.0)
        statics[SEA, 1, at, :] = sea
        for f in range(4):
            statics[f + 1, 1, at, :] = fields[f]
        state = [sea * unpack_state(arrived, rows, f, b, start[f, at, :]) for f in range(3)]
        height[1, at, :] = state[0]
        east[0, 1, at, :] = state[1]
        north[0, 1, at, :] = state[2]
        flux[1, inner(b), :] = fields[1] * state[2]

    lax.fori_loop(0, STEPS, functools.partial(forward, 1), 0)

    lost = 2 * STEPS
    outer = (lane < lost) | (lane >= LANES - lost)

    def whole(body, edges):
        return jnp.where(outer, jnp.where(slot == 0, turned(edges, 2), edges), body)

    def edges_from(body, edges):
        inward = (lane >= 2 * RIM + lost) & (lane < LANES - lost)
        return jnp.where(inward, own_edges(body), edges)

    start_copy.wait_recv()
    for b in range(blocks):
        at = span(b)
        sea = statics[SEA, 0, at, :]
        for f in range(3):
            ends = [
                height[half, at, :] if f == 0 else (east, north)[f - 1][STEPS, half, at, :]
                for half in range(2)
            ]
            defect[f, at, :] = sea * (whole(*ends) - next_start[f, at, :])
    behind_copy = pltpu.make_async_remote_copy(
        src_ref=defect,
        dst_ref=behind,
        send_sem=behind_send,
        recv_sem=behind_recv,
        device_id=(ahead, cell),
        device_id_type=MESH,
    )
    behind_copy.start()
    defect_store = pltpu.make_async_copy(defect, defect_out.at[0], out_sem.at[0])
    defect_store.start()

    for relay in relays:
        relay.wait_recv()
    for b in range(blocks):
        at = span(b)
        for half in range(2):
            keep = statics[KEEP, half, at, :]
            misses = []
            for f in range(3):
                miss = defect[f, at, :]
                if half == 1:
                    end = height[1, at, :] if f == 0 else (east, north)[f - 1][STEPS, 1, at, :]
                    target = unpack_state(next_rim, 0, f, b, next_start[f, at, :])
                    miss = edges_from(miss, statics[SEA, 1, at, :] * (end - target))
                misses.append(miss)
            east_part = keep * misses[1]
            north_part = keep * misses[2]
            height[half, at, :] = misses[0]
            adjoint_east[half, at, :] = east_part
            flux[half, inner(b), :] = north_part
            total[half, at, :] = (
                east_part * east[STEPS, half, at, :] + north_part * north[STEPS, half, at, :]
            )

    def adjoint_height(half):
        for b in range(blocks):
            at = span(b)
            slope = across(adjoint_east[half, at, :]) + along(flux, half, b)
            new = statics[SEA, half, at, :] * (height[half, at, :] + (0.5 * PRESS_RATE) * slope)
            height[half, at, :] = new
            press[half, inner(b), :] = new

    def adjoint_flow(half, b):
        at = span(b)
        turn = rotation[at, :]
        depth = statics[DEPTH, half, at, :]
        east_part = adjoint_east[half, at, :]
        north_part = flux[half, inner(b), :]
        slope = across(press[half, inner(b), :])
        return (
            east_part - turn * north_part + depth * slope,
            north_part + turn * east_part + depth * along(press, half, b),
        )

    def adjoint(i, carry):
        n = STEPS - 1 - i
        for half in range(2):
            adjoint_height(half)
        for half in range(2):
            for b in range(blocks):
                at = span(b)
                east_new, north_new = adjoint_flow(half, b)
                keep = statics[KEEP, half, at, :]
                east_new = keep * east_new
                north_new = keep * north_new
                adjoint_east[half, at, :] = east_new
                flux[half, inner(b), :] = north_new
                total[half, at, :] = total[half, at, :] + (
                    east_new * east[n, half, at, :] + north_new * north[n, half, at, :]
                )
        return carry

    lax.fori_loop(0, STEPS - 1, adjoint, 0)

    for b in range(blocks):
        at = span(b)
        total[0, at, :] = whole(total[0, at, :], total[1, at, :])
    share = rows // slices
    for t in range(slices):
        shares[t] = total[0, t * share : (t + 1) * share, :]
    share_copies = []
    for step in range(1, slices):
        peer = lax.rem(me + step, slices)
        share_copies.append(
            pltpu.make_async_remote_copy(
                src_ref=shares.at[peer],
                dst_ref=share_in.at[step],
                send_sem=share_send.at[step],
                recv_sem=share_recv.at[step],
                device_id=(peer, cell),
                device_id_type=MESH,
            )
        )
    for copy in share_copies:
        copy.start()

    for half in range(2):
        adjoint_height(half)
    behind_copy.wait_recv()
    for b in range(blocks):
        at = span(b)
        sea = statics[SEA, 0, at, :]
        body = adjoint_flow(0, b)
        edges = adjoint_flow(1, b)
        grad[0, at, :] = whole(height[0, at, :], height[1, at, :]) - behind[0, at, :]
        for f in range(2):
            grad[f + 1, at, :] = sea * whole(body[f], edges[f]) - behind[f + 1, at, :]
    grad_store = pltpu.make_async_copy(grad, grad_out.at[0], out_sem.at[1])
    grad_store.start()

    summed = shares[me]
    for step in range(1, slices):
        share_copies[step - 1].wait_recv()
        summed = summed + share_in[step]
    share_out[...] = summed * (-1.0 / slices)
    drag_store = pltpu.make_async_copy(share_out, drag_out, out_sem.at[2])
    drag_store.start()

    for copy in halos + [start_copy] + relays + [behind_copy] + share_copies:
        copy.wait_send()
    defect_store.wait()
    grad_store.wait()
    drag_store.wait()


def handed_over(*refs):
    sems = refs[6]
    copies = [pltpu.make_async_copy(refs[i], refs[3 + i], sems.at[i]) for i in range(3)]
    for copy in copies:
        copy.start()
    for copy in copies:
        copy.wait()


def local(slices, cells, start_states, ocean_mask, depth_class, class_depth, drag_rate, tide_cos, tide_sin):
    rows, lanes = ocean_mask.shape
    assert lanes == LANES and rows == 4 * BLOCK and rows % slices == 0
    share = rows // slices

    def f32(*shape):
        return pltpu.VMEM(shape, jnp.float32)

    sems = pltpu.SemaphoreType.DMA
    hbm = pl.BlockSpec(memory_space=pl.ANY)
    wide = rows + 2 * PAD
    rim_rows = rows - BLOCK
    results = pl.pallas_call(
        functools.partial(kernel, slices, cells),
        out_shape=(
            jax.ShapeDtypeStruct(start_states.shape, jnp.float32),
            jax.ShapeDtypeStruct(start_states.shape, jnp.float32),
            jax.ShapeDtypeStruct((share, lanes), jnp.float32),
        ),
        in_specs=[hbm, hbm, hbm, pl.BlockSpec(memory_space=pltpu.SMEM), hbm, hbm, hbm],
        out_specs=(hbm, hbm, hbm),
        scratch_shapes=[
            f32(3, rows, lanes),
            pltpu.VMEM((rows, lanes), jnp.int32),
            pltpu.VMEM((rows, lanes), jnp.int32),
            f32(rows, lanes),
            f32(2, rows, lanes),
            f32(5, 2, rows, lanes),
            f32(rows, lanes),
            f32(2 * STEPS, lanes),
            f32(2, rows, lanes),
            f32(STEPS + 1, 2, rows, lanes),
            f32(STEPS + 1, 2, rows, lanes),
            f32(2, rows, lanes),
            f32(2, wide, lanes),
            f32(2, wide, lanes),
            f32(2, rows + rim_rows, lanes),
            f32(2, rows + rim_rows, lanes),
            f32(2, rim_rows, lanes),
            f32(3, rows, lanes),
            f32(3, rows, lanes),
            f32(3, rows, lanes),
            f32(3, rows, lanes),
            f32(2, rows, lanes),
            f32(slices, share, lanes),
            f32(slices, share, lanes),
            f32(share, lanes),
            sems((6,)),
            sems((3,)),
            sems((2,)),
            sems((2,)),
            sems,
            sems,
            sems((2,)),
            sems((2,)),
            sems,
            sems,
            sems((slices,)),
            sems((slices,)),
        ],
        compiler_params=pltpu.CompilerParams(
            collective_id=0, has_side_effects=True, vmem_limit_bytes=60 * 1024 * 1024
        ),
    )(start_states, ocean_mask, depth_class, class_depth, drag_rate, tide_cos, tide_sin)
    return pl.pallas_call(
        handed_over,
        out_shape=tuple(jax.ShapeDtypeStruct(r.shape, r.dtype) for r in results),
        in_specs=[hbm] * 3,
        out_specs=(hbm,) * 3,
        scratch_shapes=[sems((3,))],
        compiler_params=pltpu.CompilerParams(vmem_limit_bytes=60 * 1024 * 1024),
    )(*results)


def solution(mesh):
    return jax.shard_map(
        functools.partial(local, mesh.shape["tm"], mesh.shape["cell"]),
        mesh=mesh,
        in_specs=(
            P("tm", None, None, "cell"),
            P(None, "cell"),
            P(None, "cell"),
            P(),
            P(None, "cell"),
            P(None, "cell"),
            P(None, "cell"),
        ),
        out_specs=(P("tm", None, None, "cell"), P("tm", None, None, "cell"), P("tm", "cell")),
        check_vma=False,
    )
```

```python
import functools
import math

import jax
import jax.numpy as jnp
from jax import lax
from jax.experimental import pallas as pl
from jax.experimental.pallas import tpu as pltpu
from jax.sharding import PartitionSpec as P

STEPS = 8
FLUX_RATE = 0.7
PRESS_RATE = 0.7
ROTATION_RATE = 0.15

LANES = 128
RIM = 4 * STEPS
PAD = 8
BLOCK = 32
MESH = pl.DeviceIdType.MESH

SEA, KEEP, DEPTH, COS, SIN = range(5)


def kernel(
    slices,
    cells,
    start_ref,
    mask_ref,
    class_ref,
    depths_ref,
    drag_ref,
    cos_ref,
    sin_ref,
    defect_out,
    grad_out,
    drag_out,
    start,
    mask,
    classes,
    table,
    drag,
    tides,
    statics,
    rotation,
    trig,
    height,
    east,
    north,
    adjoint_east,
    flux,
    press,
    packed,
    arrived,
    next_rim,
    next_start,
    defect,
    behind,
    grad,
    total,
    shares,
    share_in,
    share_out,
    in_sem,
    out_sem,
    piece_send,
    piece_recv,
    halo_send,
    halo_recv,
    next_send,
    next_recv,
    rim_send,
    rim_recv,
    behind_send,
    behind_recv,
    share_send,
    share_recv,
):
    rows = mask.shape[0]
    blocks = rows // BLOCK
    me = lax.axis_index("tm")
    cell = lax.axis_index("cell")
    ahead = lax.rem(me + 1, slices)
    back = lax.rem(me + slices - 1, slices)
    east_cell = lax.rem(cell + 1, cells)
    west_cell = lax.rem(cell + cells - 1, cells)

    barrier = pltpu.get_barrier_semaphore()
    for other in (west_cell, east_cell):
        pl.semaphore_signal(barrier, inc=1, device_id=(me, other), device_id_type=MESH)
    for step in range(1, slices):
        peer = lax.rem(me + step, slices)
        pl.semaphore_signal(barrier, inc=1, device_id=(peer, cell), device_id_type=MESH)

    loads = [
        pltpu.make_async_copy(source, target, in_sem.at[i])
        for i, (source, target) in enumerate(
            (
                (mask_ref, mask),
                (class_ref, classes),
                (depths_ref, table),
                (drag_ref, drag),
                (cos_ref, tides.at[0]),
                (sin_ref, tides.at[1]),
                (start_ref.at[0], start),
            )
        )
    ]
    for load in loads:
        load.start()
    for load in loads:
        load.wait()

    lane = lax.broadcasted_iota(jnp.int32, (BLOCK, LANES), 1)
    slot = lane // RIM

    def span(b):
        return pl.ds(b * BLOCK, BLOCK)

    def across(value):
        return pltpu.roll(value, LANES - 1, 1) - pltpu.roll(value, 1, 1)

    def along(ref, half, b):
        upper = ref[half, pl.ds(PAD + b * BLOCK + 1, BLOCK), :]
        lower = ref[half, pl.ds(PAD + b * BLOCK - 1, BLOCK), :]
        return upper - lower

    def inner(b):
        return pl.ds(PAD + b * BLOCK, BLOCK)

    def turned(value, by):
        return value if by % 4 == 0 else pltpu.roll(value, by % 4 * RIM, 1)

    def pack(parts):
        west = parts[0]
        east_side = turned(parts[0], 2)
        for f in range(1, 4):
            west = jnp.where(slot == f, turned(parts[f], f), west)
            east_side = jnp.where(slot == (f + 1) % 4, turned(parts[f], f - 2), east_side)
        return west, east_side

    def own_edges(value):
        return jnp.where(slot == 3, value, turned(value, 2))

    for b in range(blocks):
        at = span(b)
        sea = mask[at, :].astype(jnp.float32)
        depth = jnp.zeros((BLOCK, LANES), jnp.float32)
        kind = classes[at, :]
        for c in range(table.shape[0]):
            depth = jnp.where(kind == c, table[c], depth)
        depth = (0.5 * FLUX_RATE) * depth
        keep = sea / (1.0 + drag[at, :])
        cosine = (0.5 * PRESS_RATE) * tides[0, at, :]
        sine = (0.5 * PRESS_RATE) * tides[1, at, :]
        fields = (sea, keep, depth, cosine, sine)
        for f in range(5):
            statics[f, 0, at, :] = fields[f]
        west, east_side = pack(fields[1:])
        packed[0, at, :] = west
        packed[1, at, :] = east_side
    for b in range(blocks - 1):
        parts = [start[f, span(b), :] for f in range(3)]
        parts.append(start[b, span(blocks - 1), :])
        west, east_side = pack(parts)
        packed[0, pl.ds(rows + b * BLOCK, BLOCK), :] = west
        packed[1, pl.ds(rows + b * BLOCK, BLOCK), :] = east_side

    pl.semaphore_wait(barrier, slices + 1)

    group = math.gcd(slices, 8)
    piece = rows // group
    rank = lax.rem(me, group)
    piece_rows = pl.ds(pl.multiple_of(rank * piece, piece), piece)
    sides = ((0, west_cell), (1, east_cell))
    pieces = [
        pltpu.make_async_remote_copy(
            src_ref=packed.at[side, piece_rows],
            dst_ref=arrived.at[side, piece_rows],
            send_sem=piece_send.at[side, 0],
            recv_sem=piece_recv.at[side, 0],
            device_id=(me, other),
            device_id_type=MESH,
        )
        for side, other in sides
    ]
    state_rows = pl.ds(rows, rows - BLOCK)
    halos = [
        pltpu.make_async_remote_copy(
            src_ref=packed.at[side, state_rows],
            dst_ref=arrived.at[side, state_rows],
            send_sem=halo_send.at[side],
            recv_sem=halo_recv.at[side],
            device_id=(me, other),
            device_id_type=MESH,
        )
        for side, other in sides
    ]
    for copy in pieces + halos:
        copy.start()
    start_copy = pltpu.make_async_remote_copy(
        src_ref=start,
        dst_ref=next_start,
        send_sem=next_send,
        recv_sem=next_recv,
        device_id=(back, cell),
        device_id_type=MESH,
    )
    start_copy.start()

    latitude = lax.broadcasted_iota(jnp.int32, (rows, LANES), 0).astype(jnp.float32)
    latitude = math.pi * ((latitude + 0.5) / rows - 0.5)
    rotation[...] = ROTATION_RATE * jnp.sin(latitude)
    unit = 2.0 * math.pi / (slices * STEPS)
    number = lax.broadcasted_iota(jnp.int32, (STEPS, LANES), 0) + me * STEPS
    phase = number.astype(jnp.float32) * unit
    trig[0:STEPS, :] = jnp.cos(phase)
    trig[STEPS : 2 * STEPS, :] = jnp.sin(phase)
    blank = jnp.zeros((PAD, LANES), jnp.float32)
    for ref in (flux, press):
        for half in range(2):
            ref[half, 0:PAD, :] = blank
            ref[half, PAD + rows : 2 * PAD + rows, :] = blank
    for b in range(blocks):
        at = span(b)
        sea = statics[SEA, 0, at, :]
        height[0, at, :] = sea * start[0, at, :]
        east[0, 0, at, :] = sea * start[1, at, :]
        north_now = sea * start[2, at, :]
        north[0, 0, at, :] = north_now
        flux[0, inner(b), :] = statics[DEPTH, 0, at, :] * north_now

    def forward(half, n, carry):
        cosine = trig[pl.ds(n, 1), :]
        sine = trig[pl.ds(STEPS + n, 1), :]
        for b in range(blocks):
            at = span(b)
            spread = across(statics[DEPTH, half, at, :] * east[n, half, at, :])
            new = statics[SEA, half, at, :] * (
                height[half, at, :] - (spread + along(flux, half, b))
            )
            height[half, at, :] = new
            press[half, inner(b), :] = (0.5 * PRESS_RATE) * new + (
                cosine * statics[COS, half, at, :] + sine * statics[SIN, half, at, :]
            )
        for b in range(blocks):
            at = span(b)
            turn = rotation[at, :]
            east_now = east[n, half, at, :]
            north_now = north[n, half, at, :]
            keep = statics[KEEP, half, at, :]
            north_new = keep * (north_now - along(press, half, b) - turn * east_now)
            east[n + 1, half, at, :] = keep * (
                east_now - across(press[half, inner(b), :]) + turn * north_now
            )
            north[n + 1, half, at, :] = north_new
            flux[half, inner(b), :] = statics[DEPTH, half, at, :] * north_new
        return carry

    shared = []
    for side in range(2):
        pieces[side].wait_recv()
        for step in range(1, group):
            shared.append(
                pltpu.make_async_remote_copy(
                    src_ref=arrived.at[side, piece_rows],
                    dst_ref=arrived.at[side, piece_rows],
                    send_sem=piece_send.at[side, step],
                    recv_sem=piece_recv.at[side, step],
                    device_id=(me - rank + lax.rem(rank + step, group), cell),
                    device_id_type=MESH,
                )
            )
            shared[-1].start()

    lax.fori_loop(0, STEPS, functools.partial(forward, 0), 0)

    for halo in halos:
        halo.wait_recv()
    relays = [
        pltpu.make_async_remote_copy(
            src_ref=arrived.at[side, pl.ds(rows, rows - BLOCK)],
            dst_ref=next_rim.at[side],
            send_sem=rim_send.at[side],
            recv_sem=rim_recv.at[side],
            device_id=(back, cell),
            device_id_type=MESH,
        )
        for side in range(2)
    ]
    for relay in relays:
        relay.start()

    for copy in shared:
        copy.wait_recv()

    def unpack(ref, at, f, own):
        rims = turned(
            jnp.where(slot == f, ref[0, at, :], ref[1, at, :]),
            -f,
        )
        return jnp.where(slot < 2, rims, own_edges(own))

    def unpack_state(ref, offset, f, b, own):
        if b < blocks - 1:
            return unpack(ref, pl.ds(offset + b * BLOCK, BLOCK), f, own)
        return unpack(ref, pl.ds(offset + f * BLOCK, BLOCK), 3, own)

    for b in range(blocks):
        at = span(b)
        fields = [unpack(arrived, at, f, statics[f + 1, 0, at, :]) for f in range(4)]
        sea = jnp.where(fields[0] > 0.0, 1.0, 0.0)
        statics[SEA, 1, at, :] = sea
        for f in range(4):
            statics[f + 1, 1, at, :] = fields[f]
        state = [sea * unpack_state(arrived, rows, f, b, start[f, at, :]) for f in range(3)]
        height[1, at, :] = state[0]
        east[0, 1, at, :] = state[1]
        north[0, 1, at, :] = state[2]
        flux[1, inner(b), :] = fields[1] * state[2]

    lax.fori_loop(0, STEPS, functools.partial(forward, 1), 0)

    lost = 2 * STEPS
    outer = (lane < lost) | (lane >= LANES - lost)

    def whole(body, edges):
        return jnp.where(outer, jnp.where(slot == 0, turned(edges, 2), edges), body)

    def edges_from(body, edges):
        inward = (lane >= 2 * RIM + lost) & (lane < LANES - lost)
        return jnp.where(inward, own_edges(body), edges)

    start_copy.wait_recv()
    for b in range(blocks):
        at = span(b)
        sea = statics[SEA, 0, at, :]
        for f in range(3):
            ends = [
                height[half, at, :] if f == 0 else (east, north)[f - 1][STEPS, half, at, :]
                for half in range(2)
            ]
            defect[f, at, :] = sea * (whole(*ends) - next_start[f, at, :])
    behind_copy = pltpu.make_async_remote_copy(
        src_ref=defect,
        dst_ref=behind,
        send_sem=behind_send,
        recv_sem=behind_recv,
        device_id=(ahead, cell),
        device_id_type=MESH,
    )
    behind_copy.start()
    defect_store = pltpu.make_async_copy(defect, defect_out.at[0], out_sem.at[0])
    defect_store.start()

    for relay in relays:
        relay.wait_recv()
    for b in range(blocks):
        at = span(b)
        for half in range(2):
            keep = statics[KEEP, half, at, :]
            misses = []
            for f in range(3):
                miss = defect[f, at, :]
                if half == 1:
                    end = height[1, at, :] if f == 0 else (east, north)[f - 1][STEPS, 1, at, :]
                    target = unpack_state(next_rim, 0, f, b, next_start[f, at, :])
                    miss = edges_from(miss, statics[SEA, 1, at, :] * (end - target))
                misses.append(miss)
            east_part = keep * misses[1]
            north_part = keep * misses[2]
            height[half, at, :] = misses[0]
            adjoint_east[half, at, :] = east_part
            flux[half, inner(b), :] = north_part
            total[half, at, :] = (
                east_part * east[STEPS, half, at, :] + north_part * north[STEPS, half, at, :]
            )

    def adjoint_height(half):
        for b in range(blocks):
            at = span(b)
            slope = across(adjoint_east[half, at, :]) + along(flux, half, b)
            new = statics[SEA, half, at, :] * (height[half, at, :] + (0.5 * PRESS_RATE) * slope)
            height[half, at, :] = new
            press[half, inner(b), :] = new

    def adjoint_flow(half, b):
        at = span(b)
        turn = rotation[at, :]
        depth = statics[DEPTH, half, at, :]
        east_part = adjoint_east[half, at, :]
        north_part = flux[half, inner(b), :]
        slope = across(press[half, inner(b), :])
        return (
            east_part - turn * north_part + depth * slope,
            north_part + turn * east_part + depth * along(press, half, b),
        )

    def adjoint(i, carry):
        n = STEPS - 1 - i
        for half in range(2):
            adjoint_height(half)
        for half in range(2):
            for b in range(blocks):
                at = span(b)
                east_new, north_new = adjoint_flow(half, b)
                keep = statics[KEEP, half, at, :]
                east_new = keep * east_new
                north_new = keep * north_new
                adjoint_east[half, at, :] = east_new
                flux[half, inner(b), :] = north_new
                total[half, at, :] = total[half, at, :] + (
                    east_new * east[n, half, at, :] + north_new * north[n, half, at, :]
                )
        return carry

    lax.fori_loop(0, STEPS - 1, adjoint, 0)

    for b in range(blocks):
        at = span(b)
        total[0, at, :] = whole(total[0, at, :], total[1, at, :])
    share = rows // slices
    for t in range(slices):
        shares[t] = total[0, t * share : (t + 1) * share, :]
    share_copies = []
    for step in range(1, slices):
        peer = lax.rem(me + step, slices)
        share_copies.append(
            pltpu.make_async_remote_copy(
                src_ref=shares.at[peer],
                dst_ref=share_in.at[step],
                send_sem=share_send.at[step],
                recv_sem=share_recv.at[step],
                device_id=(peer, cell),
                device_id_type=MESH,
            )
        )
    for copy in share_copies:
        copy.start()

    for half in range(2):
        adjoint_height(half)
    behind_copy.wait_recv()
    for b in range(blocks):
        at = span(b)
        sea = statics[SEA, 0, at, :]
        body = adjoint_flow(0, b)
        edges = adjoint_flow(1, b)
        grad[0, at, :] = whole(height[0, at, :], height[1, at, :]) - behind[0, at, :]
        for f in range(2):
            grad[f + 1, at, :] = sea * whole(body[f], edges[f]) - behind[f + 1, at, :]
    grad_store = pltpu.make_async_copy(grad, grad_out.at[0], out_sem.at[1])
    grad_store.start()

    summed = shares[me]
    for step in range(1, slices):
        share_copies[step - 1].wait_recv()
        summed = summed + share_in[step]
    share_out[...] = summed * (-1.0 / slices)
    drag_store = pltpu.make_async_copy(share_out, drag_out, out_sem.at[2])
    drag_store.start()

    for copy in pieces + shared + halos + [start_copy] + relays + [behind_copy] + share_copies:
        copy.wait_send()
    defect_store.wait()
    grad_store.wait()
    drag_store.wait()


def handed_over(*refs):
    sems = refs[6]
    copies = [pltpu.make_async_copy(refs[i], refs[3 + i], sems.at[i]) for i in range(3)]
    for copy in copies:
        copy.start()
    for copy in copies:
        copy.wait()


def local(slices, cells, *operands):
    start_states, ocean_mask, _, class_depth = operands[:4]
    rows, lanes = ocean_mask.shape
    assert lanes == LANES and rows == 4 * BLOCK and rows % slices == 0
    share = rows // slices

    def f32(*shape):
        return pltpu.VMEM(shape, jnp.float32)

    sems = pltpu.SemaphoreType.DMA
    hbm = pl.BlockSpec(memory_space=pltpu.HBM)
    left = pl.BlockSpec(memory_space=pl.ANY)
    wide = rows + 2 * PAD
    rim_rows = rows - BLOCK
    results = pl.pallas_call(
        functools.partial(kernel, slices, cells),
        out_shape=(f32(*start_states.shape), f32(*start_states.shape), f32(share, lanes)),
        in_specs=[hbm] * 7,
        out_specs=(left,) * 3,
        scratch_shapes=[
            f32(3, rows, lanes),
            pltpu.VMEM((rows, lanes), jnp.int32),
            pltpu.VMEM((rows, lanes), jnp.int32),
            pltpu.SMEM(class_depth.shape, jnp.float32),
            f32(rows, lanes),
            f32(2, rows, lanes),
            f32(5, 2, rows, lanes),
            f32(rows, lanes),
            f32(2 * STEPS, lanes),
            f32(2, rows, lanes),
            f32(STEPS + 1, 2, rows, lanes),
            f32(STEPS + 1, 2, rows, lanes),
            f32(2, rows, lanes),
            f32(2, wide, lanes),
            f32(2, wide, lanes),
            f32(2, rows + rim_rows, lanes),
            f32(2, rows + rim_rows, lanes),
            f32(2, rim_rows, lanes),
            f32(3, rows, lanes),
            f32(3, rows, lanes),
            f32(3, rows, lanes),
            f32(3, rows, lanes),
            f32(2, rows, lanes),
            f32(slices, share, lanes),
            f32(slices, share, lanes),
            f32(share, lanes),
            sems((7,)),
            sems((3,)),
            sems((2, math.gcd(slices, 8))),
            sems((2, math.gcd(slices, 8))),
            sems((2,)),
            sems((2,)),
            sems,
            sems,
            sems((2,)),
            sems((2,)),
            sems,
            sems,
            sems((slices,)),
            sems((slices,)),
        ],
        compiler_params=pltpu.CompilerParams(
            collective_id=0, has_side_effects=True, vmem_limit_bytes=32 * 1024 * 1024
        ),
    )(
        *(pltpu.with_memory_space_constraint(x, pltpu.HBM) for x in operands),
    )
    return pl.pallas_call(
        handed_over,
        out_shape=tuple(jax.ShapeDtypeStruct(r.shape, r.dtype) for r in results),
        in_specs=[left] * 3,
        out_specs=(hbm,) * 3,
        scratch_shapes=[sems((3,))],
        compiler_params=pltpu.CompilerParams(vmem_limit_bytes=16 * 1024 * 1024),
    )(*results)


def solution(mesh):
    return jax.shard_map(
        functools.partial(local, mesh.shape["tm"], mesh.shape["cell"]),
        mesh=mesh,
        in_specs=(
            P("tm", None, None, "cell"),
            P(None, "cell"),
            P(None, "cell"),
            P(),
            P(None, "cell"),
            P(None, "cell"),
            P(None, "cell"),
        ),
        out_specs=(P("tm", None, None, "cell"), P("tm", None, None, "cell"), P("tm", "cell")),
        check_vma=False,
    )
```

```python
import functools
import math

import jax
import jax.numpy as jnp
from jax import lax
from jax.experimental import pallas as pl
from jax.experimental.pallas import tpu as pltpu
from jax.sharding import PartitionSpec as P

STEPS = 8
FLUX_RATE = 0.7
PRESS_RATE = 0.7
ROTATION_RATE = 0.15

SCALE = 0.5 * PRESS_RATE

LANES = 128
RIM = 4 * STEPS
PAD = 8
BLOCK = 32
MESH = pl.DeviceIdType.MESH

SEA, KEEP, DEPTH, COS, SIN = range(5)


def kernel(
    slices,
    cells,
    start_ref,
    mask_ref,
    class_ref,
    depths_ref,
    drag_ref,
    cos_ref,
    sin_ref,
    defect_out,
    grad_out,
    drag_out,
    start,
    mask,
    classes,
    table,
    drag,
    tides,
    statics,
    rotation,
    trig,
    height,
    east,
    north,
    adjoint_east,
    flux,
    press,
    packed,
    arrived,
    own_rim,
    next_rim,
    next_start,
    defect,
    behind,
    grad,
    total,
    shares,
    share_in,
    in_sem,
    out_sem,
    piece_send,
    piece_recv,
    halo_send,
    halo_recv,
    next_send,
    next_recv,
    rim_send,
    rim_recv,
    behind_send,
    behind_recv,
    share_send,
    share_recv,
):
    rows = mask.shape[0]
    blocks = rows // BLOCK
    me = lax.axis_index("tm")
    cell = lax.axis_index("cell")
    ahead = lax.rem(me + 1, slices)
    back = lax.rem(me + slices - 1, slices)
    east_cell = lax.rem(cell + 1, cells)
    west_cell = lax.rem(cell + cells - 1, cells)

    barrier = pltpu.get_barrier_semaphore()
    for other in (west_cell, east_cell):
        pl.semaphore_signal(barrier, inc=1, device_id=(me, other), device_id_type=MESH)
    for step in range(1, slices):
        peer = lax.rem(me + step, slices)
        pl.semaphore_signal(barrier, inc=1, device_id=(peer, cell), device_id_type=MESH)

    loads = [
        pltpu.make_async_copy(source, target, in_sem.at[i])
        for i, (source, target) in enumerate(
            (
                (mask_ref, mask),
                (class_ref, classes),
                (depths_ref, table),
                (drag_ref, drag),
                (cos_ref, tides.at[0]),
                (sin_ref, tides.at[1]),
                (start_ref.at[0], start),
            )
        )
    ]
    for load in loads:
        load.start()

    lane = lax.broadcasted_iota(jnp.int32, (BLOCK, LANES), 1)
    slot = lane // RIM

    def span(b):
        return pl.ds(b * BLOCK, BLOCK)

    def across(value):
        return pltpu.roll(value, LANES - 1, 1) - pltpu.roll(value, 1, 1)

    def along(ref, half, b):
        upper = ref[half, pl.ds(PAD + b * BLOCK + 1, BLOCK), :]
        lower = ref[half, pl.ds(PAD + b * BLOCK - 1, BLOCK), :]
        return upper - lower

    def inner(b):
        return pl.ds(PAD + b * BLOCK, BLOCK)

    def turned(value, by):
        return value if by % 4 == 0 else pltpu.roll(value, by % 4 * RIM, 1)

    def pack(parts):
        west = parts[0]
        east_side = turned(parts[0], 2)
        for f in range(1, 4):
            west = jnp.where(slot == f, turned(parts[f], f), west)
            east_side = jnp.where(slot == (f + 1) % 4, turned(parts[f], f - 2), east_side)
        return west, east_side

    def own_edges(value):
        return jnp.where(slot == 3, value, turned(value, 2))

    loads[-1].wait()
    for b in range(blocks - 1):
        parts = [start[f, span(b), :] for f in range(3)]
        parts.append(start[b, span(blocks - 1), :])
        west, east_side = pack(parts)
        packed[0, pl.ds(rows + b * BLOCK, BLOCK), :] = west
        packed[1, pl.ds(rows + b * BLOCK, BLOCK), :] = east_side

    for load in loads[:-1]:
        load.wait()
    for b in range(blocks):
        at = span(b)
        sea = mask[at, :].astype(jnp.float32)
        depth = jnp.zeros((BLOCK, LANES), jnp.float32)
        kind = classes[at, :]
        for c in range(table.shape[0]):
            depth = jnp.where(kind == c, table[c], depth)
        depth = (0.5 * FLUX_RATE * SCALE) * depth
        keep = sea / (1.0 + drag[at, :])
        cosine = tides[0, at, :]
        sine = tides[1, at, :]
        fields = (sea, keep, depth, cosine, sine)
        for f in range(5):
            statics[f, 0, at, :] = fields[f]
        west, east_side = pack(fields[1:])
        packed[0, at, :] = west
        packed[1, at, :] = east_side
    pl.semaphore_wait(barrier, slices + 1)

    group = math.gcd(slices, 8)
    piece = rows // group
    rank = lax.rem(me, group)
    piece_rows = pl.ds(pl.multiple_of(rank * piece, piece), piece)
    sides = ((0, west_cell), (1, east_cell))
    pieces = [
        pltpu.make_async_remote_copy(
            src_ref=packed.at[side, piece_rows],
            dst_ref=arrived.at[side, piece_rows],
            send_sem=piece_send.at[side, 0],
            recv_sem=piece_recv.at[side, 0],
            device_id=(me, other),
            device_id_type=MESH,
        )
        for side, other in sides
    ]
    state_rows = pl.ds(rows, rows - BLOCK)
    halos = [
        pltpu.make_async_remote_copy(
            src_ref=packed.at[side, state_rows],
            dst_ref=arrived.at[side, state_rows],
            send_sem=halo_send.at[side],
            recv_sem=halo_recv.at[side],
            device_id=(me, other),
            device_id_type=MESH,
        )
        for side, other in sides
    ]
    for copy in pieces + halos:
        copy.start()
    start_copy = pltpu.make_async_remote_copy(
        src_ref=start,
        dst_ref=next_start,
        send_sem=next_send,
        recv_sem=next_recv,
        device_id=(back, cell),
        device_id_type=MESH,
    )
    start_copy.start()

    latitude = lax.broadcasted_iota(jnp.int32, (rows, LANES), 0).astype(jnp.float32)
    latitude = math.pi * ((latitude + 0.5) / rows - 0.5)
    rotation[...] = ROTATION_RATE * jnp.sin(latitude)
    unit = 2.0 * math.pi / (slices * STEPS)
    number = lax.broadcasted_iota(jnp.int32, (STEPS, LANES), 0) + me * STEPS
    phase = number.astype(jnp.float32) * unit
    trig[0:STEPS, :] = jnp.cos(phase)
    trig[STEPS : 2 * STEPS, :] = jnp.sin(phase)
    blank = jnp.zeros((PAD, LANES), jnp.float32)
    for ref in (flux, press):
        for half in range(2):
            ref[half, 0:PAD, :] = blank
            ref[half, PAD + rows : 2 * PAD + rows, :] = blank
    for b in range(blocks):
        at = span(b)
        sea = statics[SEA, 0, at, :]
        height[0, at, :] = sea * start[0, at, :]
        speed = (1.0 / SCALE) * sea
        east[0, 0, at, :] = speed * start[1, at, :]
        north_now = speed * start[2, at, :]
        north[0, 0, at, :] = north_now
        flux[0, inner(b), :] = statics[DEPTH, 0, at, :] * north_now

    def forward(half, n):
        cosine = trig[n : n + 1, :]
        sine = trig[STEPS + n : STEPS + n + 1, :]
        for b in range(blocks):
            at = span(b)
            spread = across(statics[DEPTH, half, at, :] * east[n, half, at, :])
            new = statics[SEA, half, at, :] * (
                height[half, at, :] - (spread + along(flux, half, b))
            )
            height[half, at, :] = new
            press[half, inner(b), :] = new + (
                cosine * statics[COS, half, at, :] + sine * statics[SIN, half, at, :]
            )
        for b in range(blocks):
            at = span(b)
            turn = rotation[at, :]
            east_now = east[n, half, at, :]
            north_now = north[n, half, at, :]
            keep = statics[KEEP, half, at, :]
            north_new = keep * (north_now - along(press, half, b) - turn * east_now)
            east[n + 1, half, at, :] = keep * (
                east_now - across(press[half, inner(b), :]) + turn * north_now
            )
            north[n + 1, half, at, :] = north_new
            flux[half, inner(b), :] = statics[DEPTH, half, at, :] * north_new

    shared = []
    for side in range(2):
        pieces[side].wait_recv()
        for step in range(1, group):
            shared.append(
                pltpu.make_async_remote_copy(
                    src_ref=arrived.at[side, piece_rows],
                    dst_ref=arrived.at[side, piece_rows],
                    send_sem=piece_send.at[side, step],
                    recv_sem=piece_recv.at[side, step],
                    device_id=(me - rank + lax.rem(rank + step, group), cell),
                    device_id_type=MESH,
                )
            )
            shared[-1].start()

    for n in range(STEPS):
        forward(0, n)

    for copy in shared:
        copy.wait_recv()

    def unpack(ref, at, f, own):
        rims = turned(jnp.where(slot == f, ref[0, at, :], ref[1, at, :]), -f)
        return jnp.where(slot < 2, rims, own_edges(own))

    for b in range(blocks):
        at = span(b)
        fields = [unpack(arrived, at, f, statics[f + 1, 0, at, :]) for f in range(4)]
        statics[SEA, 1, at, :] = jnp.where(fields[0] > 0.0, 1.0, 0.0)
        for f in range(4):
            statics[f + 1, 1, at, :] = fields[f]

    def state_place(f, b):
        if b < blocks - 1:
            return pl.ds(b * BLOCK, BLOCK), f
        return pl.ds(f * BLOCK, BLOCK), 3

    for halo in halos:
        halo.wait_recv()
    lost = 2 * STEPS
    near_slots = []
    for f in range(3):
        offset = lax.rem(lane + (4 - f) * RIM, LANES)
        near_slots.append((offset < lost) | ((offset >= 2 * RIM - lost) & (offset < 2 * RIM)))
    edge_start = {}
    for b in range(blocks):
        for f in range(3):
            at, slot_at = state_place(f, b)
            edge_start[f, b] = unpack(
                arrived.at[:, state_rows], at, slot_at, start[f, span(b), :]
            )
    for b in range(blocks - 1):
        mixed = turned(edge_start[b, blocks - 1], 3)
        for f in range(3):
            mixed = jnp.where(near_slots[f], turned(edge_start[f, b], f), mixed)
        own_rim[span(b), :] = mixed
    relay = pltpu.make_async_remote_copy(
        src_ref=own_rim,
        dst_ref=next_rim,
        send_sem=rim_send,
        recv_sem=rim_recv,
        device_id=(back, cell),
        device_id_type=MESH,
    )
    relay.start()
    for b in range(blocks):
        at = span(b)
        sea = statics[SEA, 1, at, :]
        speed = (1.0 / SCALE) * sea
        height[1, at, :] = sea * edge_start[0, b]
        east[0, 1, at, :] = speed * edge_start[1, b]
        north_now = speed * edge_start[2, b]
        north[0, 1, at, :] = north_now
        flux[1, inner(b), :] = statics[DEPTH, 1, at, :] * north_now

    for n in range(STEPS):
        forward(1, n)

    outer = (lane < lost) | (lane >= LANES - lost)

    def whole(body, edges):
        return jnp.where(outer, jnp.where(slot == 0, turned(edges, 2), edges), body)

    def edges_from(body, edges):
        inward = (lane >= 2 * RIM + lost) & (lane < LANES - lost)
        return jnp.where(inward, own_edges(body), edges)

    start_copy.wait_recv()
    for b in range(blocks):
        at = span(b)
        sea = statics[SEA, 0, at, :]
        for f in range(3):
            ends = [
                height[half, at, :] if f == 0 else SCALE * (east, north)[f - 1][STEPS, half, at, :]
                for half in range(2)
            ]
            defect[f, at, :] = sea * (whole(*ends) - next_start[f, at, :])
    behind_copy = pltpu.make_async_remote_copy(
        src_ref=defect,
        dst_ref=behind,
        send_sem=behind_send,
        recv_sem=behind_recv,
        device_id=(ahead, cell),
        device_id_type=MESH,
    )
    behind_copy.start()
    defect_store = pltpu.make_async_copy(defect, defect_out.at[0], out_sem.at[0])
    defect_store.start()

    relay.wait_recv()
    for b in range(blocks):
        at = span(b)
        for half in range(2):
            keep = SCALE * statics[KEEP, half, at, :]
            misses = []
            for f in range(3):
                miss = defect[f, at, :]
                if half == 1:
                    end = height[1, at, :]
                    if f > 0:
                        end = SCALE * (east, north)[f - 1][STEPS, 1, at, :]
                    place, slot_at = state_place(f, b)
                    target = jnp.where(
                        slot < 2,
                        turned(next_rim[place, :], -slot_at),
                        own_edges(next_start[f, at, :]),
                    )
                    miss = edges_from(miss, statics[SEA, 1, at, :] * (end - target))
                misses.append(miss)
            east_part = keep * misses[1]
            north_part = keep * misses[2]
            height[half, at, :] = misses[0]
            adjoint_east[half, at, :] = east_part
            flux[half, inner(b), :] = north_part
            total[half, at, :] = (
                east_part * east[STEPS, half, at, :] + north_part * north[STEPS, half, at, :]
            )

    def adjoint_height(half):
        for b in range(blocks):
            at = span(b)
            slope = across(adjoint_east[half, at, :]) + along(flux, half, b)
            new = statics[SEA, half, at, :] * (height[half, at, :] + slope)
            height[half, at, :] = new
            press[half, inner(b), :] = new

    def adjoint_flow(half, b):
        at = span(b)
        turn = rotation[at, :]
        depth = statics[DEPTH, half, at, :]
        east_part = adjoint_east[half, at, :]
        north_part = flux[half, inner(b), :]
        slope = across(press[half, inner(b), :])
        return (
            east_part - turn * north_part + depth * slope,
            north_part + turn * east_part + depth * along(press, half, b),
        )

    def adjoint(n):
        for half in range(2):
            adjoint_height(half)
        for half in range(2):
            for b in range(blocks):
                at = span(b)
                east_new, north_new = adjoint_flow(half, b)
                keep = statics[KEEP, half, at, :]
                east_new = keep * east_new
                north_new = keep * north_new
                adjoint_east[half, at, :] = east_new
                flux[half, inner(b), :] = north_new
                total[half, at, :] = total[half, at, :] + (
                    east_new * east[n, half, at, :] + north_new * north[n, half, at, :]
                )

    for n in range(STEPS - 1, 0, -1):
        adjoint(n)

    for b in range(blocks):
        at = span(b)
        total[0, at, :] = whole(total[0, at, :], total[1, at, :])
    share = rows // slices
    for t in range(slices):
        shares[t] = total[0, t * share : (t + 1) * share, :]
    share_copies = []
    for step in range(1, slices):
        peer = lax.rem(me + step, slices)
        share_copies.append(
            pltpu.make_async_remote_copy(
                src_ref=shares.at[peer],
                dst_ref=share_in.at[step],
                send_sem=share_send.at[step],
                recv_sem=share_recv.at[step],
                device_id=(peer, cell),
                device_id_type=MESH,
            )
        )
    for copy in share_copies:
        copy.start()

    for half in range(2):
        adjoint_height(half)
    behind_copy.wait_recv()
    for b in range(blocks):
        at = span(b)
        sea = (1.0 / SCALE) * statics[SEA, 0, at, :]
        body = adjoint_flow(0, b)
        edges = adjoint_flow(1, b)
        grad[0, at, :] = whole(height[0, at, :], height[1, at, :]) - behind[0, at, :]
        for f in range(2):
            grad[f + 1, at, :] = sea * whole(body[f], edges[f]) - behind[f + 1, at, :]
    grad_store = pltpu.make_async_copy(grad, grad_out.at[0], out_sem.at[1])
    grad_store.start()

    summed = shares[me]
    for step in range(1, slices):
        share_copies[step - 1].wait_recv()
        summed = summed + share_in[step]
    drag_out[...] = summed * (-1.0 / slices)

    for copy in pieces + shared + halos + [start_copy, relay, behind_copy] + share_copies:
        copy.wait_send()
    defect_store.wait()
    grad_store.wait()


def handed_over(*refs):
    sems = refs[6]
    copies = [pltpu.make_async_copy(refs[i], refs[3 + i], sems.at[i]) for i in range(3)]
    for copy in copies:
        copy.start()
    for copy in copies:
        copy.wait()


def local(slices, cells, *operands):
    start_states, ocean_mask, _, class_depth = operands[:4]
    rows, lanes = ocean_mask.shape
    assert lanes == LANES and rows == 4 * BLOCK and rows % slices == 0
    share = rows // slices

    def f32(*shape):
        return pltpu.VMEM(shape, jnp.float32)

    sems = pltpu.SemaphoreType.DMA
    hbm = pl.BlockSpec(memory_space=pltpu.HBM)
    left = pl.BlockSpec(memory_space=pl.ANY)
    wide = rows + 2 * PAD
    rim_rows = rows - BLOCK
    results = pl.pallas_call(
        functools.partial(kernel, slices, cells),
        out_shape=(f32(*start_states.shape), f32(*start_states.shape), f32(share, lanes)),
        in_specs=[hbm] * 7,
        out_specs=(left, left, pl.BlockSpec(memory_space=pltpu.VMEM)),
        scratch_shapes=[
            f32(3, rows, lanes),
            pltpu.VMEM((rows, lanes), jnp.int32),
            pltpu.VMEM((rows, lanes), jnp.int32),
            pltpu.SMEM(class_depth.shape, jnp.float32),
            f32(rows, lanes),
            f32(2, rows, lanes),
            f32(5, 2, rows, lanes),
            f32(rows, lanes),
            f32(2 * STEPS, lanes),
            f32(2, rows, lanes),
            f32(STEPS + 1, 2, rows, lanes),
            f32(STEPS + 1, 2, rows, lanes),
            f32(2, rows, lanes),
            f32(2, wide, lanes),
            f32(2, wide, lanes),
            f32(2, rows + rim_rows, lanes),
            f32(2, rows + rim_rows, lanes),
            f32(rim_rows, lanes),
            f32(rim_rows, lanes),
            f32(3, rows, lanes),
            f32(3, rows, lanes),
            f32(3, rows, lanes),
            f32(3, rows, lanes),
            f32(2, rows, lanes),
            f32(slices, share, lanes),
            f32(slices, share, lanes),
            sems((7,)),
            sems((2,)),
            sems((2, math.gcd(slices, 8))),
            sems((2, math.gcd(slices, 8))),
            sems((2,)),
            sems((2,)),
            sems,
            sems,
            sems,
            sems,
            sems,
            sems,
            sems((slices,)),
            sems((slices,)),
        ],
        compiler_params=pltpu.CompilerParams(
            collective_id=0, has_side_effects=True, vmem_limit_bytes=32 * 1024 * 1024
        ),
    )(
        *(pltpu.with_memory_space_constraint(x, pltpu.HBM) for x in operands),
    )
    return pl.pallas_call(
        handed_over,
        out_shape=tuple(jax.ShapeDtypeStruct(r.shape, r.dtype) for r in results),
        in_specs=[left] * 3,
        out_specs=(hbm,) * 3,
        scratch_shapes=[sems((3,))],
        compiler_params=pltpu.CompilerParams(vmem_limit_bytes=16 * 1024 * 1024),
    )(*results)


def solution(mesh):
    return jax.shard_map(
        functools.partial(local, mesh.shape["tm"], mesh.shape["cell"]),
        mesh=mesh,
        in_specs=(
            P("tm", None, None, "cell"),
            P(None, "cell"),
            P(None, "cell"),
            P(),
            P(None, "cell"),
            P(None, "cell"),
            P(None, "cell"),
        ),
        out_specs=(P("tm", None, None, "cell"), P("tm", None, None, "cell"), P("tm", "cell")),
        check_vma=False,
    )
```

```python
import functools
import math

import jax
import jax.numpy as jnp
import numpy as np
from jax import lax
from jax.experimental import pallas as pl
from jax.experimental.pallas import tpu as pltpu
from jax.sharding import PartitionSpec as P

STEPS = 8
FLUX_RATE = 0.7
PRESS_RATE = 0.7
ROTATION_RATE = 0.15

SCALE = 0.5 * PRESS_RATE

LANES = 128
RIM = 4 * STEPS
PAD = 8
BLOCK = 32
MESH = pl.DeviceIdType.MESH

SEA, KEEP, DEPTH, COS, SIN = range(5)


def kernel(
    slices,
    cells,
    start_ref,
    mask_ref,
    class_ref,
    depths_ref,
    drag_ref,
    cos_ref,
    sin_ref,
    rotation_ref,
    defect_out,
    grad_out,
    drag_out,
    start,
    mask,
    classes,
    table,
    drag,
    tides,
    statics,
    rotation,
    trig,
    height,
    east,
    north,
    adjoint_east,
    flux,
    press,
    packed,
    arrived,
    own_rim,
    next_rim,
    next_start,
    defect,
    behind,
    grad,
    total,
    shares,
    share_in,
    in_sem,
    out_sem,
    piece_send,
    piece_recv,
    halo_send,
    halo_recv,
    next_send,
    next_recv,
    rim_send,
    rim_recv,
    behind_send,
    behind_recv,
    share_send,
    share_recv,
):
    rows = mask.shape[0]
    blocks = rows // BLOCK
    me = lax.axis_index("tm")
    cell = lax.axis_index("cell")
    ahead = lax.rem(me + 1, slices)
    back = lax.rem(me + slices - 1, slices)
    east_cell = lax.rem(cell + 1, cells)
    west_cell = lax.rem(cell + cells - 1, cells)

    barrier = pltpu.get_barrier_semaphore()
    for other in (west_cell, east_cell):
        pl.semaphore_signal(barrier, inc=1, device_id=(me, other), device_id_type=MESH)
    for step in range(1, slices):
        peer = lax.rem(me + step, slices)
        pl.semaphore_signal(barrier, inc=1, device_id=(peer, cell), device_id_type=MESH)

    loads = [
        pltpu.make_async_copy(source, target, in_sem.at[i])
        for i, (source, target) in enumerate(
            (
                (mask_ref, mask),
                (class_ref, classes),
                (depths_ref, table),
                (drag_ref, drag),
                (cos_ref, tides.at[0]),
                (sin_ref, tides.at[1]),
                (rotation_ref, rotation),
                (start_ref.at[0], start),
            )
        )
    ]
    for load in loads:
        load.start()

    lane = lax.broadcasted_iota(jnp.int32, (BLOCK, LANES), 1)
    slot = lane // RIM

    def span(b):
        return pl.ds(b * BLOCK, BLOCK)

    def across(value):
        return pltpu.roll(value, LANES - 1, 1) - pltpu.roll(value, 1, 1)

    def along(ref, half, b):
        upper = ref[half, pl.ds(PAD + b * BLOCK + 1, BLOCK), :]
        lower = ref[half, pl.ds(PAD + b * BLOCK - 1, BLOCK), :]
        return upper - lower

    def inner(b):
        return pl.ds(PAD + b * BLOCK, BLOCK)

    def turned(value, by):
        return value if by % 4 == 0 else pltpu.roll(value, by % 4 * RIM, 1)

    def pack(parts):
        west = parts[0]
        east_side = turned(parts[0], 2)
        for f in range(1, 4):
            west = jnp.where(slot == f, turned(parts[f], f), west)
            east_side = jnp.where(slot == (f + 1) % 4, turned(parts[f], f - 2), east_side)
        return west, east_side

    def own_edges(value):
        return jnp.where(slot == 3, value, turned(value, 2))

    loads[-1].wait()
    for b in range(blocks - 1):
        parts = [start[f, span(b), :] for f in range(3)]
        parts.append(start[b, span(blocks - 1), :])
        west, east_side = pack(parts)
        packed[0, pl.ds(rows + b * BLOCK, BLOCK), :] = west
        packed[1, pl.ds(rows + b * BLOCK, BLOCK), :] = east_side

    for load in loads[:-1]:
        load.wait()
    for b in range(blocks):
        at = span(b)
        sea = mask[at, :].astype(jnp.float32)
        depth = jnp.zeros((BLOCK, LANES), jnp.float32)
        kind = classes[at, :]
        for c in range(table.shape[0]):
            depth = jnp.where(kind == c, table[c], depth)
        depth = (0.5 * FLUX_RATE * SCALE) * depth
        keep = sea / (1.0 + drag[at, :])
        cosine = tides[0, at, :]
        sine = tides[1, at, :]
        fields = (sea, keep, depth, cosine, sine)
        for f in range(5):
            statics[f, 0, at, :] = fields[f]
        west, east_side = pack(fields[1:])
        packed[0, at, :] = west
        packed[1, at, :] = east_side
    pl.semaphore_wait(barrier, slices + 1)

    group = math.gcd(slices, 8)
    piece = rows // group
    rank = lax.rem(me, group)
    piece_rows = pl.ds(pl.multiple_of(rank * piece, piece), piece)
    sides = ((0, west_cell), (1, east_cell))
    pieces = [
        pltpu.make_async_remote_copy(
            src_ref=packed.at[side, piece_rows],
            dst_ref=arrived.at[side, piece_rows],
            send_sem=piece_send.at[side, 0],
            recv_sem=piece_recv.at[side, 0],
            device_id=(me, other),
            device_id_type=MESH,
        )
        for side, other in sides
    ]
    state_rows = pl.ds(rows, rows - BLOCK)
    halos = [
        pltpu.make_async_remote_copy(
            src_ref=packed.at[side, state_rows],
            dst_ref=arrived.at[side, state_rows],
            send_sem=halo_send.at[side],
            recv_sem=halo_recv.at[side],
            device_id=(me, other),
            device_id_type=MESH,
        )
        for side, other in sides
    ]
    for copy in pieces + halos:
        copy.start()
    start_copy = pltpu.make_async_remote_copy(
        src_ref=start,
        dst_ref=next_start,
        send_sem=next_send,
        recv_sem=next_recv,
        device_id=(back, cell),
        device_id_type=MESH,
    )

    shared = []
    for side in range(2):
        pieces[side].wait_recv()
        for step in range(1, group):
            shared.append(
                pltpu.make_async_remote_copy(
                    src_ref=arrived.at[side, piece_rows],
                    dst_ref=arrived.at[side, piece_rows],
                    send_sem=piece_send.at[side, step],
                    recv_sem=piece_recv.at[side, step],
                    device_id=(me - rank + lax.rem(rank + step, group), cell),
                    device_id_type=MESH,
                )
            )
            shared[-1].start()
    start_copy.start()

    unit = 2.0 * math.pi / (slices * STEPS)
    number = lax.broadcasted_iota(jnp.int32, (STEPS, LANES), 0) + me * STEPS
    phase = number.astype(jnp.float32) * unit
    trig[0:STEPS, :] = jnp.cos(phase)
    trig[STEPS : 2 * STEPS, :] = jnp.sin(phase)
    blank = jnp.zeros((PAD, LANES), jnp.float32)
    for ref in (flux, press):
        for half in range(2):
            ref[half, 0:PAD, :] = blank
            ref[half, PAD + rows : 2 * PAD + rows, :] = blank
    for b in range(blocks):
        at = span(b)
        sea = statics[SEA, 0, at, :]
        height[0, at, :] = sea * start[0, at, :]
        speed = (1.0 / SCALE) * sea
        east[0, 0, at, :] = speed * start[1, at, :]
        north_now = speed * start[2, at, :]
        north[0, 0, at, :] = north_now
        flux[0, inner(b), :] = statics[DEPTH, 0, at, :] * north_now

    def forward(half, n):
        cosine = trig[n : n + 1, :]
        sine = trig[STEPS + n : STEPS + n + 1, :]
        for b in range(blocks):
            at = span(b)
            spread = across(statics[DEPTH, half, at, :] * east[n, half, at, :])
            new = statics[SEA, half, at, :] * (
                height[half, at, :] - (spread + along(flux, half, b))
            )
            height[half, at, :] = new
            press[half, inner(b), :] = new + (
                cosine * statics[COS, half, at, :] + sine * statics[SIN, half, at, :]
            )
        for b in range(blocks):
            at = span(b)
            turn = rotation[at, :]
            east_now = east[n, half, at, :]
            north_now = north[n, half, at, :]
            keep = statics[KEEP, half, at, :]
            north_new = keep * (north_now - along(press, half, b) - turn * east_now)
            east[n + 1, half, at, :] = keep * (
                east_now - across(press[half, inner(b), :]) + turn * north_now
            )
            north[n + 1, half, at, :] = north_new
            flux[half, inner(b), :] = statics[DEPTH, half, at, :] * north_new

    for n in range(STEPS):
        forward(0, n)

    for copy in shared:
        copy.wait_recv()

    def unpack(ref, at, f, own):
        rims = turned(jnp.where(slot == f, ref[0, at, :], ref[1, at, :]), -f)
        return jnp.where(slot < 2, rims, own_edges(own))

    for b in range(blocks):
        at = span(b)
        fields = [unpack(arrived, at, f, statics[f + 1, 0, at, :]) for f in range(4)]
        statics[SEA, 1, at, :] = jnp.where(fields[0] > 0.0, 1.0, 0.0)
        for f in range(4):
            statics[f + 1, 1, at, :] = fields[f]

    def state_place(f, b):
        if b < blocks - 1:
            return pl.ds(b * BLOCK, BLOCK), f
        return pl.ds(f * BLOCK, BLOCK), 3

    for halo in halos:
        halo.wait_recv()
    lost = 2 * STEPS
    near_slots = []
    for f in range(3):
        offset = lax.rem(lane + (4 - f) * RIM, LANES)
        near_slots.append((offset < lost) | ((offset >= 2 * RIM - lost) & (offset < 2 * RIM)))
    edge_start = {}
    for b in range(blocks):
        for f in range(3):
            at, slot_at = state_place(f, b)
            edge_start[f, b] = unpack(
                arrived.at[:, state_rows], at, slot_at, start[f, span(b), :]
            )
    for b in range(blocks - 1):
        mixed = turned(edge_start[b, blocks - 1], 3)
        for f in range(3):
            mixed = jnp.where(near_slots[f], turned(edge_start[f, b], f), mixed)
        own_rim[span(b), :] = mixed
    relay = pltpu.make_async_remote_copy(
        src_ref=own_rim,
        dst_ref=next_rim,
        send_sem=rim_send,
        recv_sem=rim_recv,
        device_id=(back, cell),
        device_id_type=MESH,
    )
    relay.start()
    for b in range(blocks):
        at = span(b)
        sea = statics[SEA, 1, at, :]
        speed = (1.0 / SCALE) * sea
        height[1, at, :] = sea * edge_start[0, b]
        east[0, 1, at, :] = speed * edge_start[1, b]
        north_now = speed * edge_start[2, b]
        north[0, 1, at, :] = north_now
        flux[1, inner(b), :] = statics[DEPTH, 1, at, :] * north_now

    for n in range(STEPS):
        forward(1, n)

    outer = (lane < lost) | (lane >= LANES - lost)

    def whole(body, edges):
        return jnp.where(outer, jnp.where(slot == 0, turned(edges, 2), edges), body)

    def edges_from(body, edges):
        inward = (lane >= 2 * RIM + lost) & (lane < LANES - lost)
        return jnp.where(inward, own_edges(body), edges)

    start_copy.wait_recv()
    for b in range(blocks):
        at = span(b)
        sea = statics[SEA, 0, at, :]
        for f in range(3):
            ends = [
                height[half, at, :] if f == 0 else SCALE * (east, north)[f - 1][STEPS, half, at, :]
                for half in range(2)
            ]
            defect[f, at, :] = sea * (whole(*ends) - next_start[f, at, :])
    behind_copy = pltpu.make_async_remote_copy(
        src_ref=defect,
        dst_ref=behind,
        send_sem=behind_send,
        recv_sem=behind_recv,
        device_id=(ahead, cell),
        device_id_type=MESH,
    )
    behind_copy.start()
    defect_store = pltpu.make_async_copy(defect, defect_out.at[0], out_sem.at[0])
    defect_store.start()

    relay.wait_recv()
    for b in range(blocks):
        at = span(b)
        for half in range(2):
            keep = SCALE * statics[KEEP, half, at, :]
            misses = []
            for f in range(3):
                miss = defect[f, at, :]
                if half == 1:
                    end = height[1, at, :]
                    if f > 0:
                        end = SCALE * (east, north)[f - 1][STEPS, 1, at, :]
                    place, slot_at = state_place(f, b)
                    target = jnp.where(
                        slot < 2,
                        turned(next_rim[place, :], -slot_at),
                        own_edges(next_start[f, at, :]),
                    )
                    miss = edges_from(miss, statics[SEA, 1, at, :] * (end - target))
                misses.append(miss)
            east_part = keep * misses[1]
            north_part = keep * misses[2]
            height[half, at, :] = misses[0]
            adjoint_east[half, at, :] = east_part
            flux[half, inner(b), :] = north_part
            total[half, at, :] = (
                east_part * east[STEPS, half, at, :] + north_part * north[STEPS, half, at, :]
            )

    def adjoint_height(half):
        for b in range(blocks):
            at = span(b)
            slope = across(adjoint_east[half, at, :]) + along(flux, half, b)
            new = statics[SEA, half, at, :] * (height[half, at, :] + slope)
            height[half, at, :] = new
            press[half, inner(b), :] = new

    def adjoint_flow(half, b):
        at = span(b)
        turn = rotation[at, :]
        depth = statics[DEPTH, half, at, :]
        east_part = adjoint_east[half, at, :]
        north_part = flux[half, inner(b), :]
        slope = across(press[half, inner(b), :])
        return (
            east_part - turn * north_part + depth * slope,
            north_part + turn * east_part + depth * along(press, half, b),
        )

    def adjoint(n):
        for half in range(2):
            adjoint_height(half)
        for half in range(2):
            for b in range(blocks):
                at = span(b)
                east_new, north_new = adjoint_flow(half, b)
                keep = statics[KEEP, half, at, :]
                east_new = keep * east_new
                north_new = keep * north_new
                adjoint_east[half, at, :] = east_new
                flux[half, inner(b), :] = north_new
                total[half, at, :] = total[half, at, :] + (
                    east_new * east[n, half, at, :] + north_new * north[n, half, at, :]
                )

    for n in range(STEPS - 1, 0, -1):
        adjoint(n)

    for b in range(blocks):
        at = span(b)
        total[0, at, :] = whole(total[0, at, :], total[1, at, :])
    share = rows // slices
    for t in range(slices):
        shares[t] = total[0, t * share : (t + 1) * share, :]
    share_copies = []
    for step in range(1, slices):
        peer = lax.rem(me + step, slices)
        share_copies.append(
            pltpu.make_async_remote_copy(
                src_ref=shares.at[peer],
                dst_ref=share_in.at[step],
                send_sem=share_send.at[step],
                recv_sem=share_recv.at[step],
                device_id=(peer, cell),
                device_id_type=MESH,
            )
        )
    for copy in share_copies:
        copy.start()

    for half in range(2):
        adjoint_height(half)
    behind_copy.wait_recv()
    for b in range(blocks):
        at = span(b)
        sea = (1.0 / SCALE) * statics[SEA, 0, at, :]
        body = adjoint_flow(0, b)
        edges = adjoint_flow(1, b)
        grad[0, at, :] = whole(height[0, at, :], height[1, at, :]) - behind[0, at, :]
        for f in range(2):
            grad[f + 1, at, :] = sea * whole(body[f], edges[f]) - behind[f + 1, at, :]
    grad_store = pltpu.make_async_copy(grad, grad_out.at[0], out_sem.at[1])
    grad_store.start()

    summed = shares[me]
    for step in range(1, slices):
        share_copies[step - 1].wait_recv()
        summed = summed + share_in[step]
    drag_out[...] = summed * (-1.0 / slices)

    for copy in pieces + shared + halos + [start_copy, relay, behind_copy] + share_copies:
        copy.wait_send()
    defect_store.wait()
    grad_store.wait()


def handed_over(*refs):
    sems = refs[6]
    copies = [pltpu.make_async_copy(refs[i], refs[3 + i], sems.at[i]) for i in range(3)]
    for copy in copies:
        copy.start()
    for copy in copies:
        copy.wait()


def local(slices, cells, *operands):
    start_states, ocean_mask, _, class_depth = operands[:4]
    rows, lanes = ocean_mask.shape
    assert lanes == LANES and rows == 4 * BLOCK and rows % slices == 0
    share = rows // slices

    def f32(*shape):
        return pltpu.VMEM(shape, jnp.float32)

    sems = pltpu.SemaphoreType.DMA
    hbm = pl.BlockSpec(memory_space=pltpu.HBM)
    left = pl.BlockSpec(memory_space=pl.ANY)
    wide = rows + 2 * PAD
    rim_rows = rows - BLOCK
    latitude = np.pi * ((np.arange(rows) + 0.5) / rows - 0.5)
    turning = np.broadcast_to((ROTATION_RATE * np.sin(latitude))[:, None], (rows, lanes))
    turning = jnp.asarray(np.ascontiguousarray(turning, dtype=np.float32))
    results = pl.pallas_call(
        functools.partial(kernel, slices, cells),
        out_shape=(f32(*start_states.shape), f32(*start_states.shape), f32(share, lanes)),
        in_specs=[hbm] * 8,
        out_specs=(left, left, pl.BlockSpec(memory_space=pltpu.VMEM)),
        scratch_shapes=[
            f32(3, rows, lanes),
            pltpu.VMEM((rows, lanes), jnp.int32),
            pltpu.VMEM((rows, lanes), jnp.int32),
            pltpu.SMEM(class_depth.shape, jnp.float32),
            f32(rows, lanes),
            f32(2, rows, lanes),
            f32(5, 2, rows, lanes),
            f32(rows, lanes),
            f32(2 * STEPS, lanes),
            f32(2, rows, lanes),
            f32(STEPS + 1, 2, rows, lanes),
            f32(STEPS + 1, 2, rows, lanes),
            f32(2, rows, lanes),
            f32(2, wide, lanes),
            f32(2, wide, lanes),
            f32(2, rows + rim_rows, lanes),
            f32(2, rows + rim_rows, lanes),
            f32(rim_rows, lanes),
            f32(rim_rows, lanes),
            f32(3, rows, lanes),
            f32(3, rows, lanes),
            f32(3, rows, lanes),
            f32(3, rows, lanes),
            f32(2, rows, lanes),
            f32(slices, share, lanes),
            f32(slices, share, lanes),
            sems((8,)),
            sems((2,)),
            sems((2, math.gcd(slices, 8))),
            sems((2, math.gcd(slices, 8))),
            sems((2,)),
            sems((2,)),
            sems,
            sems,
            sems,
            sems,
            sems,
            sems,
            sems((slices,)),
            sems((slices,)),
        ],
        compiler_params=pltpu.CompilerParams(
            collective_id=0, has_side_effects=True, vmem_limit_bytes=32 * 1024 * 1024
        ),
    )(
        *(pltpu.with_memory_space_constraint(x, pltpu.HBM) for x in (*operands, turning)),
    )
    return pl.pallas_call(
        handed_over,
        out_shape=tuple(jax.ShapeDtypeStruct(r.shape, r.dtype) for r in results),
        in_specs=[left] * 3,
        out_specs=(hbm,) * 3,
        scratch_shapes=[sems((3,))],
        compiler_params=pltpu.CompilerParams(vmem_limit_bytes=16 * 1024 * 1024),
    )(*results)


def solution(mesh):
    return jax.shard_map(
        functools.partial(local, mesh.shape["tm"], mesh.shape["cell"]),
        mesh=mesh,
        in_specs=(
            P("tm", None, None, "cell"),
            P(None, "cell"),
            P(None, "cell"),
            P(),
            P(None, "cell"),
            P(None, "cell"),
            P(None, "cell"),
        ),
        out_specs=(P("tm", None, None, "cell"), P("tm", None, None, "cell"), P("tm", "cell")),
        check_vma=False,
    )
```

```python
import functools
import math

import jax
import jax.numpy as jnp
import numpy as np
from jax import lax
from jax.experimental import pallas as pl
from jax.experimental.pallas import tpu as pltpu
from jax.sharding import PartitionSpec as P

STEPS = 8
FLUX_RATE = 0.7
PRESS_RATE = 0.7
ROTATION_RATE = 0.15

SCALE = 0.5 * PRESS_RATE

LANES = 128
RIM = 4 * STEPS
PAD = 8
BLOCK = 32
MESH = pl.DeviceIdType.MESH

SEA, KEEP, DEPTH, COS, SIN = range(5)


def kernel(
    slices,
    cells,
    start_ref,
    mask_ref,
    class_ref,
    depths_ref,
    drag_ref,
    cos_ref,
    sin_ref,
    rotation_ref,
    defect_out,
    grad_out,
    drag_out,
    start,
    mask,
    classes,
    table,
    drag,
    tides,
    statics,
    rotation,
    trig,
    height,
    east,
    north,
    adjoint_east,
    flux,
    press,
    packed,
    arrived,
    own_rim,
    next_rim,
    next_start,
    defect,
    behind,
    grad,
    total,
    shares,
    share_in,
    in_sem,
    out_sem,
    piece_send,
    piece_recv,
    halo_send,
    halo_recv,
    next_send,
    next_recv,
    rim_send,
    rim_recv,
    behind_send,
    behind_recv,
    share_send,
    share_recv,
):
    rows = mask.shape[0]
    blocks = rows // BLOCK
    me = lax.axis_index("tm")
    cell = lax.axis_index("cell")
    ahead = lax.rem(me + 1, slices)
    back = lax.rem(me + slices - 1, slices)
    east_cell = lax.rem(cell + 1, cells)
    west_cell = lax.rem(cell + cells - 1, cells)

    barrier = pltpu.get_barrier_semaphore()
    for other in (west_cell, east_cell):
        pl.semaphore_signal(barrier, inc=1, device_id=(me, other), device_id_type=MESH)
    for step in range(1, slices):
        peer = lax.rem(me + step, slices)
        pl.semaphore_signal(barrier, inc=1, device_id=(peer, cell), device_id_type=MESH)

    loads = [
        pltpu.make_async_copy(source, target, in_sem.at[i])
        for i, (source, target) in enumerate(
            (
                (mask_ref, mask),
                (class_ref, classes),
                (depths_ref, table),
                (drag_ref, drag),
                (cos_ref, tides.at[0]),
                (sin_ref, tides.at[1]),
                (rotation_ref, rotation),
                (start_ref.at[0], start),
            )
        )
    ]
    for load in loads:
        load.start()

    lane = lax.broadcasted_iota(jnp.int32, (BLOCK, LANES), 1)
    slot = lane // RIM

    def span(b):
        return pl.ds(b * BLOCK, BLOCK)

    def across(value):
        return pltpu.roll(value, LANES - 1, 1) - pltpu.roll(value, 1, 1)

    def along(ref, half, b):
        upper = ref[half, pl.ds(PAD + b * BLOCK + 1, BLOCK), :]
        lower = ref[half, pl.ds(PAD + b * BLOCK - 1, BLOCK), :]
        return upper - lower

    def inner(b):
        return pl.ds(PAD + b * BLOCK, BLOCK)

    def turned(value, by):
        return value if by % 4 == 0 else pltpu.roll(value, by % 4 * RIM, 1)

    def pack(parts):
        west = parts[0]
        east_side = turned(parts[0], 2)
        for f in range(1, 4):
            west = jnp.where(slot == f, turned(parts[f], f), west)
            east_side = jnp.where(slot == (f + 1) % 4, turned(parts[f], f - 2), east_side)
        return west, east_side

    def own_edges(value):
        return jnp.where(slot == 3, value, turned(value, 2))

    loads[-1].wait()
    for b in range(blocks - 1):
        parts = [start[f, span(b), :] for f in range(3)]
        parts.append(start[b, span(blocks - 1), :])
        west, east_side = pack(parts)
        packed[0, pl.ds(rows + b * BLOCK, BLOCK), :] = west
        packed[1, pl.ds(rows + b * BLOCK, BLOCK), :] = east_side

    for load in loads[:-1]:
        load.wait()
    for b in range(blocks):
        at = span(b)
        sea = mask[at, :].astype(jnp.float32)
        depth = jnp.zeros((BLOCK, LANES), jnp.float32)
        kind = classes[at, :]
        for c in range(table.shape[0]):
            depth = jnp.where(kind == c, table[c], depth)
        depth = (0.5 * FLUX_RATE * SCALE) * depth
        keep = sea / (1.0 + drag[at, :])
        cosine = tides[0, at, :]
        sine = tides[1, at, :]
        fields = (sea, keep, depth, cosine, sine)
        for f in range(5):
            statics[f, 0, at, :] = fields[f]
        west, east_side = pack(fields[1:])
        packed[0, at, :] = west
        packed[1, at, :] = east_side
    pl.semaphore_wait(barrier, slices + 1)

    group = math.gcd(slices, 2)
    piece = rows // group
    rank = lax.rem(me, group)
    piece_rows = pl.ds(pl.multiple_of(rank * piece, piece), piece)
    sides = ((0, west_cell), (1, east_cell))
    pieces = [
        pltpu.make_async_remote_copy(
            src_ref=packed.at[side, piece_rows],
            dst_ref=arrived.at[side, piece_rows],
            send_sem=piece_send.at[side, 0],
            recv_sem=piece_recv.at[side, 0],
            device_id=(me, other),
            device_id_type=MESH,
        )
        for side, other in sides
    ]
    state_rows = pl.ds(rows, rows - BLOCK)
    halos = [
        pltpu.make_async_remote_copy(
            src_ref=packed.at[side, state_rows],
            dst_ref=arrived.at[side, state_rows],
            send_sem=halo_send.at[side],
            recv_sem=halo_recv.at[side],
            device_id=(me, other),
            device_id_type=MESH,
        )
        for side, other in sides
    ]
    for copy in pieces + halos:
        copy.start()
    start_copy = pltpu.make_async_remote_copy(
        src_ref=start,
        dst_ref=next_start,
        send_sem=next_send,
        recv_sem=next_recv,
        device_id=(back, cell),
        device_id_type=MESH,
    )

    shared = []
    for side in range(2):
        pieces[side].wait_recv()
        for step in range(1, group):
            shared.append(
                pltpu.make_async_remote_copy(
                    src_ref=arrived.at[side, piece_rows],
                    dst_ref=arrived.at[side, piece_rows],
                    send_sem=piece_send.at[side, step],
                    recv_sem=piece_recv.at[side, step],
                    device_id=(me - rank + lax.rem(rank + step, group), cell),
                    device_id_type=MESH,
                )
            )
            shared[-1].start()
    start_copy.start()

    unit = 2.0 * math.pi / (slices * STEPS)
    number = lax.broadcasted_iota(jnp.int32, (STEPS, LANES), 0) + me * STEPS
    phase = number.astype(jnp.float32) * unit
    trig[0:STEPS, :] = jnp.cos(phase)
    trig[STEPS : 2 * STEPS, :] = jnp.sin(phase)
    blank = jnp.zeros((PAD, LANES), jnp.float32)
    for ref in (flux, press):
        for half in range(2):
            ref[half, 0:PAD, :] = blank
            ref[half, PAD + rows : 2 * PAD + rows, :] = blank
    for b in range(blocks):
        at = span(b)
        sea = statics[SEA, 0, at, :]
        height[0, at, :] = sea * start[0, at, :]
        speed = (1.0 / SCALE) * sea
        east[0, 0, at, :] = speed * start[1, at, :]
        north_now = speed * start[2, at, :]
        north[0, 0, at, :] = north_now
        flux[0, inner(b), :] = statics[DEPTH, 0, at, :] * north_now

    def forward(half, n):
        cosine = trig[n : n + 1, :]
        sine = trig[STEPS + n : STEPS + n + 1, :]
        for b in range(blocks):
            at = span(b)
            spread = across(statics[DEPTH, half, at, :] * east[n, half, at, :])
            new = statics[SEA, half, at, :] * (
                height[half, at, :] - (spread + along(flux, half, b))
            )
            height[half, at, :] = new
            press[half, inner(b), :] = new + (
                cosine * statics[COS, half, at, :] + sine * statics[SIN, half, at, :]
            )
        for b in range(blocks):
            at = span(b)
            turn = rotation[at, :]
            east_now = east[n, half, at, :]
            north_now = north[n, half, at, :]
            keep = statics[KEEP, half, at, :]
            north_new = keep * (north_now - along(press, half, b) - turn * east_now)
            east[n + 1, half, at, :] = keep * (
                east_now - across(press[half, inner(b), :]) + turn * north_now
            )
            north[n + 1, half, at, :] = north_new
            flux[half, inner(b), :] = statics[DEPTH, half, at, :] * north_new

    for n in range(STEPS):
        forward(0, n)

    for copy in shared:
        copy.wait_recv()

    def unpack(ref, at, f, own):
        rims = turned(jnp.where(slot == f, ref[0, at, :], ref[1, at, :]), -f)
        return jnp.where(slot < 2, rims, own_edges(own))

    for b in range(blocks):
        at = span(b)
        fields = [unpack(arrived, at, f, statics[f + 1, 0, at, :]) for f in range(4)]
        statics[SEA, 1, at, :] = jnp.where(fields[0] > 0.0, 1.0, 0.0)
        for f in range(4):
            statics[f + 1, 1, at, :] = fields[f]

    def state_place(f, b):
        if b < blocks - 1:
            return pl.ds(b * BLOCK, BLOCK), f
        return pl.ds(f * BLOCK, BLOCK), 3

    for halo in halos:
        halo.wait_recv()
    lost = 2 * STEPS
    near_slots = []
    for f in range(3):
        offset = lax.rem(lane + (4 - f) * RIM, LANES)
        near_slots.append((offset < lost) | ((offset >= 2 * RIM - lost) & (offset < 2 * RIM)))
    edge_start = {}
    for b in range(blocks):
        for f in range(3):
            at, slot_at = state_place(f, b)
            edge_start[f, b] = unpack(
                arrived.at[:, state_rows], at, slot_at, start[f, span(b), :]
            )
    for b in range(blocks - 1):
        mixed = turned(edge_start[b, blocks - 1], 3)
        for f in range(3):
            mixed = jnp.where(near_slots[f], turned(edge_start[f, b], f), mixed)
        own_rim[span(b), :] = mixed
    relay = pltpu.make_async_remote_copy(
        src_ref=own_rim,
        dst_ref=next_rim,
        send_sem=rim_send,
        recv_sem=rim_recv,
        device_id=(back, cell),
        device_id_type=MESH,
    )
    relay.start()
    for b in range(blocks):
        at = span(b)
        sea = statics[SEA, 1, at, :]
        speed = (1.0 / SCALE) * sea
        height[1, at, :] = sea * edge_start[0, b]
        east[0, 1, at, :] = speed * edge_start[1, b]
        north_now = speed * edge_start[2, b]
        north[0, 1, at, :] = north_now
        flux[1, inner(b), :] = statics[DEPTH, 1, at, :] * north_now

    for n in range(STEPS):
        forward(1, n)

    outer = (lane < lost) | (lane >= LANES - lost)

    def whole(body, edges):
        return jnp.where(outer, jnp.where(slot == 0, turned(edges, 2), edges), body)

    def edges_from(body, edges):
        inward = (lane >= 2 * RIM + lost) & (lane < LANES - lost)
        return jnp.where(inward, own_edges(body), edges)

    start_copy.wait_recv()
    for b in range(blocks):
        at = span(b)
        sea = statics[SEA, 0, at, :]
        for f in range(3):
            ends = [
                height[half, at, :] if f == 0 else SCALE * (east, north)[f - 1][STEPS, half, at, :]
                for half in range(2)
            ]
            defect[f, at, :] = sea * (whole(*ends) - next_start[f, at, :])
    behind_copy = pltpu.make_async_remote_copy(
        src_ref=defect,
        dst_ref=behind,
        send_sem=behind_send,
        recv_sem=behind_recv,
        device_id=(ahead, cell),
        device_id_type=MESH,
    )
    behind_copy.start()
    defect_store = pltpu.make_async_copy(defect, defect_out.at[0], out_sem.at[0])
    defect_store.start()

    relay.wait_recv()
    for b in range(blocks):
        at = span(b)
        for half in range(2):
            keep = SCALE * statics[KEEP, half, at, :]
            misses = []
            for f in range(3):
                miss = defect[f, at, :]
                if half == 1:
                    end = height[1, at, :]
                    if f > 0:
                        end = SCALE * (east, north)[f - 1][STEPS, 1, at, :]
                    place, slot_at = state_place(f, b)
                    target = jnp.where(
                        slot < 2,
                        turned(next_rim[place, :], -slot_at),
                        own_edges(next_start[f, at, :]),
                    )
                    miss = edges_from(miss, statics[SEA, 1, at, :] * (end - target))
                misses.append(miss)
            east_part = keep * misses[1]
            north_part = keep * misses[2]
            height[half, at, :] = misses[0]
            adjoint_east[half, at, :] = east_part
            flux[half, inner(b), :] = north_part
            total[half, at, :] = (
                east_part * east[STEPS, half, at, :] + north_part * north[STEPS, half, at, :]
            )

    def adjoint_height(half):
        for b in range(blocks):
            at = span(b)
            slope = across(adjoint_east[half, at, :]) + along(flux, half, b)
            new = statics[SEA, half, at, :] * (height[half, at, :] + slope)
            height[half, at, :] = new
            press[half, inner(b), :] = new

    def adjoint_flow(half, b):
        at = span(b)
        turn = rotation[at, :]
        depth = statics[DEPTH, half, at, :]
        east_part = adjoint_east[half, at, :]
        north_part = flux[half, inner(b), :]
        slope = across(press[half, inner(b), :])
        return (
            east_part - turn * north_part + depth * slope,
            north_part + turn * east_part + depth * along(press, half, b),
        )

    def adjoint(n):
        for half in range(2):
            adjoint_height(half)
        for half in range(2):
            for b in range(blocks):
                at = span(b)
                east_new, north_new = adjoint_flow(half, b)
                keep = statics[KEEP, half, at, :]
                east_new = keep * east_new
                north_new = keep * north_new
                adjoint_east[half, at, :] = east_new
                flux[half, inner(b), :] = north_new
                total[half, at, :] = total[half, at, :] + (
                    east_new * east[n, half, at, :] + north_new * north[n, half, at, :]
                )

    for n in range(STEPS - 1, 0, -1):
        adjoint(n)

    for b in range(blocks):
        at = span(b)
        total[0, at, :] = whole(total[0, at, :], total[1, at, :])
    share = rows // slices
    for t in range(slices):
        shares[t] = total[0, t * share : (t + 1) * share, :]
    share_copies = []
    for step in range(1, slices):
        peer = lax.rem(me + step, slices)
        share_copies.append(
            pltpu.make_async_remote_copy(
                src_ref=shares.at[peer],
                dst_ref=share_in.at[step],
                send_sem=share_send.at[step],
                recv_sem=share_recv.at[step],
                device_id=(peer, cell),
                device_id_type=MESH,
            )
        )
    for copy in share_copies:
        copy.start()

    for half in range(2):
        adjoint_height(half)
    behind_copy.wait_recv()
    for b in range(blocks):
        at = span(b)
        sea = (1.0 / SCALE) * statics[SEA, 0, at, :]
        body = adjoint_flow(0, b)
        edges = adjoint_flow(1, b)
        grad[0, at, :] = whole(height[0, at, :], height[1, at, :]) - behind[0, at, :]
        for f in range(2):
            grad[f + 1, at, :] = sea * whole(body[f], edges[f]) - behind[f + 1, at, :]
    grad_store = pltpu.make_async_copy(grad, grad_out.at[0], out_sem.at[1])
    grad_store.start()

    summed = shares[me]
    for step in range(1, slices):
        share_copies[step - 1].wait_recv()
        summed = summed + share_in[step]
    drag_out[...] = summed * (-1.0 / slices)

    for copy in pieces + shared + halos + [start_copy, relay, behind_copy] + share_copies:
        copy.wait_send()
    defect_store.wait()
    grad_store.wait()


def handed_over(*refs):
    sems = refs[6]
    copies = [pltpu.make_async_copy(refs[i], refs[3 + i], sems.at[i]) for i in range(3)]
    for copy in copies:
        copy.start()
    for copy in copies:
        copy.wait()


def local(slices, cells, *operands):
    start_states, ocean_mask, _, class_depth = operands[:4]
    rows, lanes = ocean_mask.shape
    assert lanes == LANES and rows == 4 * BLOCK and rows % slices == 0
    share = rows // slices

    def f32(*shape):
        return pltpu.VMEM(shape, jnp.float32)

    sems = pltpu.SemaphoreType.DMA
    hbm = pl.BlockSpec(memory_space=pltpu.HBM)
    left = pl.BlockSpec(memory_space=pl.ANY)
    wide = rows + 2 * PAD
    rim_rows = rows - BLOCK
    latitude = np.pi * ((np.arange(rows) + 0.5) / rows - 0.5)
    turning = np.broadcast_to((ROTATION_RATE * np.sin(latitude))[:, None], (rows, lanes))
    turning = jnp.asarray(np.ascontiguousarray(turning, dtype=np.float32))
    results = pl.pallas_call(
        functools.partial(kernel, slices, cells),
        out_shape=(f32(*start_states.shape), f32(*start_states.shape), f32(share, lanes)),
        in_specs=[hbm] * 8,
        out_specs=(left, left, pl.BlockSpec(memory_space=pltpu.VMEM)),
        scratch_shapes=[
            f32(3, rows, lanes),
            pltpu.VMEM((rows, lanes), jnp.int32),
            pltpu.VMEM((rows, lanes), jnp.int32),
            pltpu.SMEM(class_depth.shape, jnp.float32),
            f32(rows, lanes),
            f32(2, rows, lanes),
            f32(5, 2, rows, lanes),
            f32(rows, lanes),
            f32(2 * STEPS, lanes),
            f32(2, rows, lanes),
            f32(STEPS + 1, 2, rows, lanes),
            f32(STEPS + 1, 2, rows, lanes),
            f32(2, rows, lanes),
            f32(2, wide, lanes),
            f32(2, wide, lanes),
            f32(2, rows + rim_rows, lanes),
            f32(2, rows + rim_rows, lanes),
            f32(rim_rows, lanes),
            f32(rim_rows, lanes),
            f32(3, rows, lanes),
            f32(3, rows, lanes),
            f32(3, rows, lanes),
            f32(3, rows, lanes),
            f32(2, rows, lanes),
            f32(slices, share, lanes),
            f32(slices, share, lanes),
            sems((8,)),
            sems((2,)),
            sems((2, math.gcd(slices, 2))),
            sems((2, math.gcd(slices, 2))),
            sems((2,)),
            sems((2,)),
            sems,
            sems,
            sems,
            sems,
            sems,
            sems,
            sems((slices,)),
            sems((slices,)),
        ],
        compiler_params=pltpu.CompilerParams(
            collective_id=0, has_side_effects=True, vmem_limit_bytes=32 * 1024 * 1024
        ),
    )(
        *(pltpu.with_memory_space_constraint(x, pltpu.HBM) for x in (*operands, turning)),
    )
    return pl.pallas_call(
        handed_over,
        out_shape=tuple(jax.ShapeDtypeStruct(r.shape, r.dtype) for r in results),
        in_specs=[left] * 3,
        out_specs=(hbm,) * 3,
        scratch_shapes=[sems((3,))],
        compiler_params=pltpu.CompilerParams(vmem_limit_bytes=16 * 1024 * 1024),
    )(*results)


def solution(mesh):
    return jax.shard_map(
        functools.partial(local, mesh.shape["tm"], mesh.shape["cell"]),
        mesh=mesh,
        in_specs=(
            P("tm", None, None, "cell"),
            P(None, "cell"),
            P(None, "cell"),
            P(),
            P(None, "cell"),
            P(None, "cell"),
            P(None, "cell"),
        ),
        out_specs=(P("tm", None, None, "cell"), P("tm", None, None, "cell"), P("tm", "cell")),
        check_vma=False,
    )
```

```python
import functools
import math

import jax
import jax.numpy as jnp
import numpy as np
from jax import lax
from jax.experimental import pallas as pl
from jax.experimental.pallas import tpu as pltpu
from jax.sharding import PartitionSpec as P

STEPS = 8
FLUX_RATE = 0.7
PRESS_RATE = 0.7
ROTATION_RATE = 0.15

SCALE = 0.5 * PRESS_RATE

LANES = 128
RIM = 4 * STEPS
PAD = 8
BLOCK = 32
MESH = pl.DeviceIdType.MESH

SEA, KEEP, DEPTH, COS, SIN = range(5)


def kernel(
    slices,
    cells,
    start_ref,
    mask_ref,
    class_ref,
    depths_ref,
    drag_ref,
    cos_ref,
    sin_ref,
    rotation_ref,
    defect_out,
    grad_out,
    drag_out,
    start,
    mask,
    classes,
    table,
    drag,
    tides,
    statics,
    rotation,
    trig,
    height,
    east,
    north,
    adjoint_east,
    flux,
    press,
    packed,
    arrived,
    own_rim,
    next_rim,
    next_start,
    defect,
    behind,
    grad,
    total,
    shares,
    share_in,
    in_sem,
    out_sem,
    piece_send,
    piece_recv,
    halo_send,
    halo_recv,
    next_send,
    next_recv,
    rim_send,
    rim_recv,
    behind_send,
    behind_recv,
    share_send,
    share_recv,
):
    rows = mask.shape[0]
    blocks = rows // BLOCK
    me = lax.axis_index("tm")
    cell = lax.axis_index("cell")
    ahead = lax.rem(me + 1, slices)
    back = lax.rem(me + slices - 1, slices)
    east_cell = lax.rem(cell + 1, cells)
    west_cell = lax.rem(cell + cells - 1, cells)

    barrier = pltpu.get_barrier_semaphore()
    for other in (west_cell, east_cell):
        pl.semaphore_signal(barrier, inc=1, device_id=(me, other), device_id_type=MESH)
    for step in range(1, slices):
        peer = lax.rem(me + step, slices)
        pl.semaphore_signal(barrier, inc=1, device_id=(peer, cell), device_id_type=MESH)

    loads = [
        pltpu.make_async_copy(source, target, in_sem.at[i])
        for i, (source, target) in enumerate(
            (
                (mask_ref, mask),
                (class_ref, classes),
                (depths_ref, table),
                (drag_ref, drag),
                (cos_ref, tides.at[0]),
                (sin_ref, tides.at[1]),
                (rotation_ref, rotation),
                (start_ref.at[0], start),
            )
        )
    ]
    for load in loads:
        load.start()

    lane = lax.broadcasted_iota(jnp.int32, (BLOCK, LANES), 1)
    slot = lane // RIM

    def span(b):
        return pl.ds(b * BLOCK, BLOCK)

    def across(value):
        return pltpu.roll(value, LANES - 1, 1) - pltpu.roll(value, 1, 1)

    def along(ref, half, b):
        upper = ref[half, pl.ds(PAD + b * BLOCK + 1, BLOCK), :]
        lower = ref[half, pl.ds(PAD + b * BLOCK - 1, BLOCK), :]
        return upper - lower

    def inner(b):
        return pl.ds(PAD + b * BLOCK, BLOCK)

    def turned(value, by):
        return value if by % 4 == 0 else pltpu.roll(value, by % 4 * RIM, 1)

    def pack(parts):
        lane = lax.broadcasted_iota(jnp.int32, parts[0].shape, 1)
        slot = lane // RIM
        west = parts[0]
        east_side = turned(parts[0], 2)
        for f in range(1, 4):
            west = jnp.where(slot == f, turned(parts[f], f), west)
            east_side = jnp.where(slot == (f + 1) % 4, turned(parts[f], f - 2), east_side)
        return west, east_side

    def own_edges(value):
        return jnp.where(slot == 3, value, turned(value, 2))

    def worked_out(at):
        sea = mask[at, :].astype(jnp.float32)
        kind = classes[at, :]
        depth = jnp.zeros(kind.shape, jnp.float32)
        for c in range(table.shape[0]):
            depth = jnp.where(kind == c, table[c], depth)
        keep = sea / (1.0 + drag[at, :])
        depth = (0.5 * FLUX_RATE * SCALE) * depth
        return sea, keep, depth, tides[0, at, :], tides[1, at, :]

    group = math.gcd(slices, 8)
    piece = rows // group
    rank = lax.rem(me, group)
    piece_rows = pl.ds(pl.multiple_of(rank * piece, piece), piece)
    sides = ((0, west_cell), (1, east_cell))
    for load in loads[:-1]:
        load.wait()
    packed[0, piece_rows, :], packed[1, piece_rows, :] = pack(worked_out(piece_rows)[1:])
    pl.semaphore_wait(barrier, slices + 1)

    pieces = [
        pltpu.make_async_remote_copy(
            src_ref=packed.at[side, piece_rows],
            dst_ref=arrived.at[side, piece_rows],
            send_sem=piece_send.at[side, 0],
            recv_sem=piece_recv.at[side, 0],
            device_id=(me, other),
            device_id_type=MESH,
        )
        for side, other in sides
    ]
    for copy in pieces:
        copy.start()

    loads[-1].wait()
    for b in range(blocks - 1):
        parts = [start[f, span(b), :] for f in range(3)]
        parts.append(start[b, span(blocks - 1), :])
        west, east_side = pack(parts)
        packed[0, pl.ds(rows + b * BLOCK, BLOCK), :] = west
        packed[1, pl.ds(rows + b * BLOCK, BLOCK), :] = east_side

    state_rows = pl.ds(rows, rows - BLOCK)
    halos = [
        pltpu.make_async_remote_copy(
            src_ref=packed.at[side, state_rows],
            dst_ref=arrived.at[side, state_rows],
            send_sem=halo_send.at[side],
            recv_sem=halo_recv.at[side],
            device_id=(me, other),
            device_id_type=MESH,
        )
        for side, other in sides
    ]
    for halo in halos:
        halo.start()
    for b in range(blocks):
        fields = worked_out(span(b))
        for f in range(5):
            statics[f, 0, span(b), :] = fields[f]

    start_copy = pltpu.make_async_remote_copy(
        src_ref=start,
        dst_ref=next_start,
        send_sem=next_send,
        recv_sem=next_recv,
        device_id=(back, cell),
        device_id_type=MESH,
    )

    shared = []
    for side in range(2):
        pieces[side].wait_recv()
        for step in range(1, group):
            shared.append(
                pltpu.make_async_remote_copy(
                    src_ref=arrived.at[side, piece_rows],
                    dst_ref=arrived.at[side, piece_rows],
                    send_sem=piece_send.at[side, step],
                    recv_sem=piece_recv.at[side, step],
                    device_id=(me - rank + lax.rem(rank + step, group), cell),
                    device_id_type=MESH,
                )
            )
            shared[-1].start()
    start_copy.start()

    unit = 2.0 * math.pi / (slices * STEPS)
    number = lax.broadcasted_iota(jnp.int32, (STEPS, LANES), 0) + me * STEPS
    phase = number.astype(jnp.float32) * unit
    trig[0:STEPS, :] = jnp.cos(phase)
    trig[STEPS : 2 * STEPS, :] = jnp.sin(phase)
    blank = jnp.zeros((PAD, LANES), jnp.float32)
    for ref in (flux, press):
        for half in range(2):
            ref[half, 0:PAD, :] = blank
            ref[half, PAD + rows : 2 * PAD + rows, :] = blank
    for b in range(blocks):
        at = span(b)
        sea = statics[SEA, 0, at, :]
        height[0, at, :] = sea * start[0, at, :]
        speed = (1.0 / SCALE) * sea
        east[0, 0, at, :] = speed * start[1, at, :]
        north_now = speed * start[2, at, :]
        north[0, 0, at, :] = north_now
        flux[0, inner(b), :] = statics[DEPTH, 0, at, :] * north_now

    def forward(half, n, carry):
        cosine = trig[pl.ds(n, 1), :]
        sine = trig[pl.ds(STEPS + n, 1), :]
        for b in range(blocks):
            at = span(b)
            spread = across(statics[DEPTH, half, at, :] * east[n, half, at, :])
            new = statics[SEA, half, at, :] * (
                height[half, at, :] - (spread + along(flux, half, b))
            )
            height[half, at, :] = new
            press[half, inner(b), :] = new + (
                cosine * statics[COS, half, at, :] + sine * statics[SIN, half, at, :]
            )
        results = []
        for b in range(blocks):
            at = span(b)
            turn = rotation[at, :]
            east_now = east[n, half, at, :]
            north_now = north[n, half, at, :]
            keep = statics[KEEP, half, at, :]
            north_new = keep * (north_now - along(press, half, b) - turn * east_now)
            east_new = keep * (east_now - across(press[half, inner(b), :]) + turn * north_now)
            results.append((east_new, north_new, statics[DEPTH, half, at, :] * north_new))
        for b in range(blocks):
            at = span(b)
            east[n + 1, half, at, :], north[n + 1, half, at, :], flux[half, inner(b), :] = results[b]
        return carry

    lax.fori_loop(0, STEPS, functools.partial(forward, 0), 0)

    for copy in shared:
        copy.wait_recv()

    def unpack(ref, at, f, own):
        rims = turned(jnp.where(slot == f, ref[0, at, :], ref[1, at, :]), -f)
        return jnp.where(slot < 2, rims, own_edges(own))

    for b in range(blocks):
        at = span(b)
        fields = [unpack(arrived, at, f, statics[f + 1, 0, at, :]) for f in range(4)]
        statics[SEA, 1, at, :] = jnp.where(fields[0] > 0.0, 1.0, 0.0)
        for f in range(4):
            statics[f + 1, 1, at, :] = fields[f]

    def state_place(f, b):
        if b < blocks - 1:
            return pl.ds(b * BLOCK, BLOCK), f
        return pl.ds(f * BLOCK, BLOCK), 3

    for halo in halos:
        halo.wait_recv()
    lost = 2 * STEPS
    near_slots = []
    for f in range(3):
        offset = lax.rem(lane + (4 - f) * RIM, LANES)
        near_slots.append((offset < lost) | ((offset >= 2 * RIM - lost) & (offset < 2 * RIM)))
    edge_start = {}
    for b in range(blocks):
        for f in range(3):
            at, slot_at = state_place(f, b)
            edge_start[f, b] = unpack(
                arrived.at[:, state_rows], at, slot_at, start[f, span(b), :]
            )
    for b in range(blocks - 1):
        mixed = turned(edge_start[b, blocks - 1], 3)
        for f in range(3):
            mixed = jnp.where(near_slots[f], turned(edge_start[f, b], f), mixed)
        own_rim[span(b), :] = mixed
    relay = pltpu.make_async_remote_copy(
        src_ref=own_rim,
        dst_ref=next_rim,
        send_sem=rim_send,
        recv_sem=rim_recv,
        device_id=(back, cell),
        device_id_type=MESH,
    )
    relay.start()
    for b in range(blocks):
        at = span(b)
        sea = statics[SEA, 1, at, :]
        speed = (1.0 / SCALE) * sea
        height[1, at, :] = sea * edge_start[0, b]
        east[0, 1, at, :] = speed * edge_start[1, b]
        north_now = speed * edge_start[2, b]
        north[0, 1, at, :] = north_now
        flux[1, inner(b), :] = statics[DEPTH, 1, at, :] * north_now

    lax.fori_loop(0, STEPS, functools.partial(forward, 1), 0)

    outer = (lane < lost) | (lane >= LANES - lost)

    def whole(body, edges):
        return jnp.where(outer, jnp.where(slot == 0, turned(edges, 2), edges), body)

    def edges_from(body, edges):
        inward = (lane >= 2 * RIM + lost) & (lane < LANES - lost)
        return jnp.where(inward, own_edges(body), edges)

    start_copy.wait_recv()
    for b in range(blocks):
        at = span(b)
        sea = statics[SEA, 0, at, :]
        for f in range(3):
            ends = [
                height[half, at, :] if f == 0 else SCALE * (east, north)[f - 1][STEPS, half, at, :]
                for half in range(2)
            ]
            defect[f, at, :] = sea * (whole(*ends) - next_start[f, at, :])
    behind_copy = pltpu.make_async_remote_copy(
        src_ref=defect,
        dst_ref=behind,
        send_sem=behind_send,
        recv_sem=behind_recv,
        device_id=(ahead, cell),
        device_id_type=MESH,
    )
    behind_copy.start()
    defect_store = pltpu.make_async_copy(defect, defect_out.at[0], out_sem.at[0])
    defect_store.start()

    relay.wait_recv()
    for b in range(blocks):
        at = span(b)
        for half in range(2):
            keep = SCALE * statics[KEEP, half, at, :]
            misses = []
            for f in range(3):
                miss = defect[f, at, :]
                if half == 1:
                    end = height[1, at, :]
                    if f > 0:
                        end = SCALE * (east, north)[f - 1][STEPS, 1, at, :]
                    place, slot_at = state_place(f, b)
                    target = jnp.where(
                        slot < 2,
                        turned(next_rim[place, :], -slot_at),
                        own_edges(next_start[f, at, :]),
                    )
                    miss = edges_from(miss, statics[SEA, 1, at, :] * (end - target))
                misses.append(miss)
            east_part = keep * misses[1]
            north_part = keep * misses[2]
            height[half, at, :] = misses[0]
            adjoint_east[half, at, :] = east_part
            flux[half, inner(b), :] = north_part
            total[half, at, :] = (
                east_part * east[STEPS, half, at, :] + north_part * north[STEPS, half, at, :]
            )

    def adjoint_height(half):
        for b in range(blocks):
            at = span(b)
            slope = across(adjoint_east[half, at, :]) + along(flux, half, b)
            new = statics[SEA, half, at, :] * (height[half, at, :] + slope)
            height[half, at, :] = new
            press[half, inner(b), :] = new

    def adjoint_flow(half, b):
        at = span(b)
        turn = rotation[at, :]
        depth = statics[DEPTH, half, at, :]
        east_part = adjoint_east[half, at, :]
        north_part = flux[half, inner(b), :]
        slope = across(press[half, inner(b), :])
        return (
            east_part - turn * north_part + depth * slope,
            north_part + turn * east_part + depth * along(press, half, b),
        )

    def adjoint(i, carry):
        n = STEPS - 1 - i
        for half in range(2):
            adjoint_height(half)
        for half in range(2):
            for b in range(blocks):
                at = span(b)
                east_new, north_new = adjoint_flow(half, b)
                keep = statics[KEEP, half, at, :]
                east_new = keep * east_new
                north_new = keep * north_new
                adjoint_east[half, at, :] = east_new
                flux[half, inner(b), :] = north_new
                total[half, at, :] = total[half, at, :] + (
                    east_new * east[n, half, at, :] + north_new * north[n, half, at, :]
                )

        return carry

    lax.fori_loop(0, STEPS - 1, adjoint, 0)

    for b in range(blocks):
        at = span(b)
        total[0, at, :] = whole(total[0, at, :], total[1, at, :])
    share = rows // slices
    for t in range(slices):
        shares[t] = total[0, t * share : (t + 1) * share, :]
    share_copies = []
    for step in range(1, slices):
        peer = lax.rem(me + step, slices)
        share_copies.append(
            pltpu.make_async_remote_copy(
                src_ref=shares.at[peer],
                dst_ref=share_in.at[step],
                send_sem=share_send.at[step],
                recv_sem=share_recv.at[step],
                device_id=(peer, cell),
                device_id_type=MESH,
            )
        )
    for copy in share_copies:
        copy.start()

    for half in range(2):
        adjoint_height(half)
    behind_copy.wait_recv()
    for b in range(blocks):
        at = span(b)
        sea = (1.0 / SCALE) * statics[SEA, 0, at, :]
        body = adjoint_flow(0, b)
        edges = adjoint_flow(1, b)
        grad[0, at, :] = whole(height[0, at, :], height[1, at, :]) - behind[0, at, :]
        for f in range(2):
            grad[f + 1, at, :] = sea * whole(body[f], edges[f]) - behind[f + 1, at, :]
    grad_store = pltpu.make_async_copy(grad, grad_out.at[0], out_sem.at[1])
    grad_store.start()

    summed = shares[me]
    for step in range(1, slices):
        share_copies[step - 1].wait_recv()
        summed = summed + share_in[step]
    drag_out[...] = summed * (-1.0 / slices)

    for copy in pieces + shared + halos + [start_copy, relay, behind_copy] + share_copies:
        copy.wait_send()
    defect_store.wait()
    grad_store.wait()


def handed_over(*refs):
    sems = refs[6]
    copies = [pltpu.make_async_copy(refs[i], refs[3 + i], sems.at[i]) for i in range(3)]
    for copy in copies:
        copy.start()
    for copy in copies:
        copy.wait()


def local(slices, cells, *operands):
    start_states, ocean_mask, _, class_depth = operands[:4]
    rows, lanes = ocean_mask.shape
    assert lanes == LANES and rows == 4 * BLOCK and rows % slices == 0
    share = rows // slices

    def f32(*shape):
        return pltpu.VMEM(shape, jnp.float32)

    sems = pltpu.SemaphoreType.DMA
    hbm = pl.BlockSpec(memory_space=pltpu.HBM)
    left = pl.BlockSpec(memory_space=pl.ANY)
    wide = rows + 2 * PAD
    rim_rows = rows - BLOCK
    latitude = np.pi * ((np.arange(rows) + 0.5) / rows - 0.5)
    turning = np.broadcast_to((ROTATION_RATE * np.sin(latitude))[:, None], (rows, lanes))
    turning = jnp.asarray(np.ascontiguousarray(turning, dtype=np.float32))
    results = pl.pallas_call(
        functools.partial(kernel, slices, cells),
        out_shape=(f32(*start_states.shape), f32(*start_states.shape), f32(share, lanes)),
        in_specs=[hbm] * 8,
        out_specs=(left, left, pl.BlockSpec(memory_space=pltpu.VMEM)),
        scratch_shapes=[
            f32(3, rows, lanes),
            pltpu.VMEM((rows, lanes), jnp.int32),
            pltpu.VMEM((rows, lanes), jnp.int32),
            pltpu.SMEM(class_depth.shape, jnp.float32),
            f32(rows, lanes),
            f32(2, rows, lanes),
            f32(5, 2, rows, lanes),
            f32(rows, lanes),
            f32(2 * STEPS, lanes),
            f32(2, rows, lanes),
            f32(STEPS + 1, 2, rows, lanes),
            f32(STEPS + 1, 2, rows, lanes),
            f32(2, rows, lanes),
            f32(2, wide, lanes),
            f32(2, wide, lanes),
            f32(2, rows + rim_rows, lanes),
            f32(2, rows + rim_rows, lanes),
            f32(rim_rows, lanes),
            f32(rim_rows, lanes),
            f32(3, rows, lanes),
            f32(3, rows, lanes),
            f32(3, rows, lanes),
            f32(3, rows, lanes),
            f32(2, rows, lanes),
            f32(slices, share, lanes),
            f32(slices, share, lanes),
            sems((8,)),
            sems((2,)),
            sems((2, math.gcd(slices, 8))),
            sems((2, math.gcd(slices, 8))),
            sems((2,)),
            sems((2,)),
            sems,
            sems,
            sems,
            sems,
            sems,
            sems,
            sems((slices,)),
            sems((slices,)),
        ],
        compiler_params=pltpu.CompilerParams(
            collective_id=0, has_side_effects=True, vmem_limit_bytes=32 * 1024 * 1024
        ),
    )(
        *(pltpu.with_memory_space_constraint(x, pltpu.HBM) for x in (*operands, turning)),
    )
    return pl.pallas_call(
        handed_over,
        out_shape=tuple(jax.ShapeDtypeStruct(r.shape, r.dtype) for r in results),
        in_specs=[left] * 3,
        out_specs=(hbm,) * 3,
        scratch_shapes=[sems((3,))],
        compiler_params=pltpu.CompilerParams(vmem_limit_bytes=16 * 1024 * 1024),
    )(*results)


def solution(mesh):
    return jax.shard_map(
        functools.partial(local, mesh.shape["tm"], mesh.shape["cell"]),
        mesh=mesh,
        in_specs=(
            P("tm", None, None, "cell"),
            P(None, "cell"),
            P(None, "cell"),
            P(),
            P(None, "cell"),
            P(None, "cell"),
            P(None, "cell"),
        ),
        out_specs=(P("tm", None, None, "cell"), P("tm", None, None, "cell"), P("tm", "cell")),
        check_vma=False,
    )
```

```python
import functools
import math

import jax
import jax.numpy as jnp
import numpy as np
from jax import lax
from jax.experimental import pallas as pl
from jax.experimental.pallas import tpu as pltpu
from jax.sharding import PartitionSpec as P

STEPS = 8
FLUX_RATE = 0.7
PRESS_RATE = 0.7
ROTATION_RATE = 0.15

SCALE = 0.5 * PRESS_RATE

LANES = 128
RIM = 4 * STEPS
PAD = 8
BLOCK = 32
MESH = pl.DeviceIdType.MESH

SEA, KEEP, DEPTH, COS, SIN = range(5)


def kernel(
    slices,
    cells,
    start_ref,
    mask_ref,
    class_ref,
    depths_ref,
    drag_ref,
    cos_ref,
    sin_ref,
    rotation_ref,
    defect_out,
    grad_out,
    drag_out,
    start,
    mask,
    classes,
    table,
    drag,
    tides,
    statics,
    rotation,
    trig,
    height,
    east,
    north,
    adjoint_east,
    flux,
    press,
    packed,
    arrived,
    own_rim,
    next_rim,
    next_start,
    defect,
    behind,
    grad,
    total,
    shares,
    share_in,
    in_sem,
    out_sem,
    piece_send,
    piece_recv,
    halo_send,
    halo_recv,
    next_send,
    next_recv,
    rim_send,
    rim_recv,
    behind_send,
    behind_recv,
    share_send,
    share_recv,
):
    rows = mask.shape[0]
    blocks = rows // BLOCK
    me = lax.axis_index("tm")
    cell = lax.axis_index("cell")
    ahead = lax.rem(me + 1, slices)
    back = lax.rem(me + slices - 1, slices)
    east_cell = lax.rem(cell + 1, cells)
    west_cell = lax.rem(cell + cells - 1, cells)

    barrier = pltpu.get_barrier_semaphore()
    for other in (west_cell, east_cell):
        pl.semaphore_signal(barrier, inc=1, device_id=(me, other), device_id_type=MESH)
    for step in range(1, slices):
        peer = lax.rem(me + step, slices)
        pl.semaphore_signal(barrier, inc=1, device_id=(peer, cell), device_id_type=MESH)

    loads = [
        pltpu.make_async_copy(source, target, in_sem.at[i])
        for i, (source, target) in enumerate(
            (
                (mask_ref, mask),
                (class_ref, classes),
                (depths_ref, table),
                (drag_ref, drag),
                (cos_ref, tides.at[0]),
                (sin_ref, tides.at[1]),
                (rotation_ref, rotation),
                (start_ref.at[0], start),
            )
        )
    ]
    for load in loads:
        load.start()

    lane = lax.broadcasted_iota(jnp.int32, (BLOCK, LANES), 1)
    slot = lane // RIM

    def span(b):
        return pl.ds(b * BLOCK, BLOCK)

    def across(value):
        return pltpu.roll(value, LANES - 1, 1) - pltpu.roll(value, 1, 1)

    def along(ref, half, b):
        upper = ref[half, pl.ds(PAD + b * BLOCK + 1, BLOCK), :]
        lower = ref[half, pl.ds(PAD + b * BLOCK - 1, BLOCK), :]
        return upper - lower

    def inner(b):
        return pl.ds(PAD + b * BLOCK, BLOCK)

    def turned(value, by):
        return value if by % 4 == 0 else pltpu.roll(value, by % 4 * RIM, 1)

    def pack(parts):
        lane = lax.broadcasted_iota(jnp.int32, parts[0].shape, 1)
        slot = lane // RIM
        west = parts[0]
        east_side = turned(parts[0], 2)
        for f in range(1, 4):
            west = jnp.where(slot == f, turned(parts[f], f), west)
            east_side = jnp.where(slot == (f + 1) % 4, turned(parts[f], f - 2), east_side)
        return west, east_side

    def own_edges(value):
        return jnp.where(slot == 3, value, turned(value, 2))

    def worked_out(at):
        sea = mask[at, :].astype(jnp.float32)
        kind = classes[at, :]
        depth = jnp.zeros(kind.shape, jnp.float32)
        for c in range(table.shape[0]):
            depth = jnp.where(kind == c, table[c], depth)
        keep = sea / (1.0 + drag[at, :])
        depth = (0.5 * FLUX_RATE * SCALE) * depth
        return sea, keep, depth, tides[0, at, :], tides[1, at, :]

    group = math.gcd(slices, 8)
    piece = rows // group
    rank = lax.rem(me, group)
    piece_rows = pl.ds(pl.multiple_of(rank * piece, piece), piece)
    sides = ((0, west_cell), (1, east_cell))
    for load in loads[:-1]:
        load.wait()
    packed[0, piece_rows, :], packed[1, piece_rows, :] = pack(worked_out(piece_rows)[1:])
    pl.semaphore_wait(barrier, slices + 1)

    pieces = [
        pltpu.make_async_remote_copy(
            src_ref=packed.at[side, piece_rows],
            dst_ref=arrived.at[side, piece_rows],
            send_sem=piece_send.at[side, 0],
            recv_sem=piece_recv.at[side, 0],
            device_id=(me, other),
            device_id_type=MESH,
        )
        for side, other in sides
    ]
    for copy in pieces:
        copy.start()

    loads[-1].wait()
    for b in range(blocks - 1):
        parts = [start[f, span(b), :] for f in range(3)]
        parts.append(start[b, span(blocks - 1), :])
        west, east_side = pack(parts)
        packed[0, pl.ds(rows + b * BLOCK, BLOCK), :] = west
        packed[1, pl.ds(rows + b * BLOCK, BLOCK), :] = east_side

    state_rows = pl.ds(rows, rows - BLOCK)
    halos = [
        pltpu.make_async_remote_copy(
            src_ref=packed.at[side, state_rows],
            dst_ref=arrived.at[side, state_rows],
            send_sem=halo_send.at[side],
            recv_sem=halo_recv.at[side],
            device_id=(me, other),
            device_id_type=MESH,
        )
        for side, other in sides
    ]
    for halo in halos:
        halo.start()
    for b in range(blocks):
        fields = worked_out(span(b))
        for f in range(5):
            statics[f, 0, span(b), :] = fields[f]

    start_copy = pltpu.make_async_remote_copy(
        src_ref=start,
        dst_ref=next_start,
        send_sem=next_send,
        recv_sem=next_recv,
        device_id=(back, cell),
        device_id_type=MESH,
    )

    shared = []
    for side in range(2):
        pieces[side].wait_recv()
        for step in range(1, group):
            shared.append(
                pltpu.make_async_remote_copy(
                    src_ref=arrived.at[side, piece_rows],
                    dst_ref=arrived.at[side, piece_rows],
                    send_sem=piece_send.at[side, step],
                    recv_sem=piece_recv.at[side, step],
                    device_id=(me - rank + lax.rem(rank + step, group), cell),
                    device_id_type=MESH,
                )
            )
            shared[-1].start()
    start_copy.start()

    unit = 2.0 * math.pi / (slices * STEPS)
    number = lax.broadcasted_iota(jnp.int32, (STEPS, LANES), 0) + me * STEPS
    phase = number.astype(jnp.float32) * unit
    trig[0:STEPS, :] = jnp.cos(phase)
    trig[STEPS : 2 * STEPS, :] = jnp.sin(phase)
    blank = jnp.zeros((PAD, LANES), jnp.float32)
    for ref in (flux, press):
        for half in range(2):
            ref[half, 0:PAD, :] = blank
            ref[half, PAD + rows : 2 * PAD + rows, :] = blank
    for b in range(blocks):
        at = span(b)
        sea = statics[SEA, 0, at, :]
        height[0, at, :] = sea * start[0, at, :]
        speed = (1.0 / SCALE) * sea
        east[0, 0, at, :] = speed * start[1, at, :]
        north_now = speed * start[2, at, :]
        north[0, 0, at, :] = north_now
        flux[0, inner(b), :] = statics[DEPTH, 0, at, :] * north_now

    def forward(half, n):
        cosine = trig[n : n + 1, :]
        sine = trig[STEPS + n : STEPS + n + 1, :]
        for b in range(blocks):
            at = span(b)
            spread = across(statics[DEPTH, half, at, :] * east[n, half, at, :])
            new = statics[SEA, half, at, :] * (
                height[half, at, :] - (spread + along(flux, half, b))
            )
            height[half, at, :] = new
            press[half, inner(b), :] = new + (
                cosine * statics[COS, half, at, :] + sine * statics[SIN, half, at, :]
            )
        for b in range(blocks):
            at = span(b)
            turn = rotation[at, :]
            east_now = east[n, half, at, :]
            north_now = north[n, half, at, :]
            keep = statics[KEEP, half, at, :]
            north_new = keep * (north_now - along(press, half, b) - turn * east_now)
            east[n + 1, half, at, :] = keep * (
                east_now - across(press[half, inner(b), :]) + turn * north_now
            )
            north[n + 1, half, at, :] = north_new
            flux[half, inner(b), :] = statics[DEPTH, half, at, :] * north_new

    for n in range(STEPS):
        forward(0, n)

    for copy in shared:
        copy.wait_recv()

    def unpack(ref, at, f, own):
        rims = turned(jnp.where(slot == f, ref[0, at, :], ref[1, at, :]), -f)
        return jnp.where(slot < 2, rims, own_edges(own))

    for b in range(blocks):
        at = span(b)
        fields = [unpack(arrived, at, f, statics[f + 1, 0, at, :]) for f in range(4)]
        statics[SEA, 1, at, :] = jnp.where(fields[0] > 0.0, 1.0, 0.0)
        for f in range(4):
            statics[f + 1, 1, at, :] = fields[f]

    def state_place(f, b):
        if b < blocks - 1:
            return pl.ds(b * BLOCK, BLOCK), f
        return pl.ds(f * BLOCK, BLOCK), 3

    for halo in halos:
        halo.wait_recv()
    lost = 2 * STEPS
    near_slots = []
    for f in range(3):
        offset = lax.rem(lane + (4 - f) * RIM, LANES)
        near_slots.append((offset < lost) | ((offset >= 2 * RIM - lost) & (offset < 2 * RIM)))
    edge_start = {}
    for b in range(blocks):
        for f in range(3):
            at, slot_at = state_place(f, b)
            edge_start[f, b] = unpack(
                arrived.at[:, state_rows], at, slot_at, start[f, span(b), :]
            )
    for b in range(blocks - 1):
        mixed = turned(edge_start[b, blocks - 1], 3)
        for f in range(3):
            mixed = jnp.where(near_slots[f], turned(edge_start[f, b], f), mixed)
        own_rim[span(b), :] = mixed
    relay = pltpu.make_async_remote_copy(
        src_ref=own_rim,
        dst_ref=next_rim,
        send_sem=rim_send,
        recv_sem=rim_recv,
        device_id=(back, cell),
        device_id_type=MESH,
    )
    relay.start()
    for b in range(blocks):
        at = span(b)
        sea = statics[SEA, 1, at, :]
        speed = (1.0 / SCALE) * sea
        height[1, at, :] = sea * edge_start[0, b]
        east[0, 1, at, :] = speed * edge_start[1, b]
        north_now = speed * edge_start[2, b]
        north[0, 1, at, :] = north_now
        flux[1, inner(b), :] = statics[DEPTH, 1, at, :] * north_now

    for n in range(STEPS):
        forward(1, n)

    outer = (lane < lost) | (lane >= LANES - lost)

    def whole(body, edges):
        return jnp.where(outer, jnp.where(slot == 0, turned(edges, 2), edges), body)

    def edges_from(body, edges):
        inward = (lane >= 2 * RIM + lost) & (lane < LANES - lost)
        return jnp.where(inward, own_edges(body), edges)

    start_copy.wait_recv()
    for b in range(blocks):
        at = span(b)
        sea = statics[SEA, 0, at, :]
        for f in range(3):
            ends = [
                height[half, at, :] if f == 0 else SCALE * (east, north)[f - 1][STEPS, half, at, :]
                for half in range(2)
            ]
            defect[f, at, :] = sea * (whole(*ends) - next_start[f, at, :])
    behind_copy = pltpu.make_async_remote_copy(
        src_ref=defect,
        dst_ref=behind,
        send_sem=behind_send,
        recv_sem=behind_recv,
        device_id=(ahead, cell),
        device_id_type=MESH,
    )
    behind_copy.start()
    defect_store = pltpu.make_async_copy(defect, defect_out.at[0], out_sem.at[0])
    defect_store.start()

    relay.wait_recv()
    for b in range(blocks):
        at = span(b)
        for half in range(2):
            keep = SCALE * statics[KEEP, half, at, :]
            misses = []
            for f in range(3):
                miss = defect[f, at, :]
                if half == 1:
                    end = height[1, at, :]
                    if f > 0:
                        end = SCALE * (east, north)[f - 1][STEPS, 1, at, :]
                    place, slot_at = state_place(f, b)
                    target = jnp.where(
                        slot < 2,
                        turned(next_rim[place, :], -slot_at),
                        own_edges(next_start[f, at, :]),
                    )
                    miss = edges_from(miss, statics[SEA, 1, at, :] * (end - target))
                misses.append(miss)
            east_part = keep * misses[1]
            north_part = keep * misses[2]
            height[half, at, :] = misses[0]
            adjoint_east[half, at, :] = east_part
            flux[half, inner(b), :] = north_part
            total[half, at, :] = (
                east_part * east[STEPS, half, at, :] + north_part * north[STEPS, half, at, :]
            )

    def adjoint_height(half):
        for b in range(blocks):
            at = span(b)
            slope = across(adjoint_east[half, at, :]) + along(flux, half, b)
            new = statics[SEA, half, at, :] * (height[half, at, :] + slope)
            height[half, at, :] = new
            press[half, inner(b), :] = new

    def adjoint_flow(half, b):
        at = span(b)
        turn = rotation[at, :]
        depth = statics[DEPTH, half, at, :]
        east_part = adjoint_east[half, at, :]
        north_part = flux[half, inner(b), :]
        slope = across(press[half, inner(b), :])
        return (
            east_part - turn * north_part + depth * slope,
            north_part + turn * east_part + depth * along(press, half, b),
        )

    def adjoint(n):
        for half in range(2):
            adjoint_height(half)
        for half in range(2):
            for b in range(blocks):
                at = span(b)
                east_new, north_new = adjoint_flow(half, b)
                keep = statics[KEEP, half, at, :]
                east_new = keep * east_new
                north_new = keep * north_new
                adjoint_east[half, at, :] = east_new
                flux[half, inner(b), :] = north_new
                total[half, at, :] = total[half, at, :] + (
                    east_new * east[n, half, at, :] + north_new * north[n, half, at, :]
                )

    for n in range(STEPS - 1, 0, -1):
        adjoint(n)

    for b in range(blocks):
        at = span(b)
        total[0, at, :] = whole(total[0, at, :], total[1, at, :])
    share = rows // slices
    for t in range(slices):
        shares[t] = total[0, t * share : (t + 1) * share, :]
    share_copies = []
    for step in range(1, slices):
        peer = lax.rem(me + step, slices)
        share_copies.append(
            pltpu.make_async_remote_copy(
                src_ref=shares.at[peer],
                dst_ref=share_in.at[step],
                send_sem=share_send.at[step],
                recv_sem=share_recv.at[step],
                device_id=(peer, cell),
                device_id_type=MESH,
            )
        )
    for copy in share_copies:
        copy.start()

    for half in range(2):
        adjoint_height(half)
    behind_copy.wait_recv()
    for b in range(blocks):
        at = span(b)
        sea = (1.0 / SCALE) * statics[SEA, 0, at, :]
        body = adjoint_flow(0, b)
        edges = adjoint_flow(1, b)
        grad[0, at, :] = whole(height[0, at, :], height[1, at, :]) - behind[0, at, :]
        for f in range(2):
            grad[f + 1, at, :] = sea * whole(body[f], edges[f]) - behind[f + 1, at, :]
    grad_store = pltpu.make_async_copy(grad, grad_out.at[0], out_sem.at[1])
    grad_store.start()

    summed = shares[me]
    for step in range(1, slices):
        share_copies[step - 1].wait_recv()
        summed = summed + share_in[step]
    drag_out[...] = summed * (-1.0 / slices)

    for copy in pieces + shared + halos + [start_copy, relay, behind_copy] + share_copies:
        copy.wait_send()
    defect_store.wait()
    grad_store.wait()


def handed_over(*refs):
    sems = refs[6]
    copies = [pltpu.make_async_copy(refs[i], refs[3 + i], sems.at[i]) for i in range(3)]
    for copy in copies:
        copy.start()
    for copy in copies:
        copy.wait()


def local(slices, cells, *operands):
    start_states, ocean_mask, _, class_depth = operands[:4]
    rows, lanes = ocean_mask.shape
    assert lanes == LANES and rows == 4 * BLOCK and rows % slices == 0
    share = rows // slices

    def f32(*shape):
        return pltpu.VMEM(shape, jnp.float32)

    sems = pltpu.SemaphoreType.DMA
    hbm = pl.BlockSpec(memory_space=pltpu.HBM)
    left = pl.BlockSpec(memory_space=pl.ANY)
    wide = rows + 2 * PAD
    rim_rows = rows - BLOCK
    latitude = np.pi * ((np.arange(rows) + 0.5) / rows - 0.5)
    turning = np.broadcast_to((ROTATION_RATE * np.sin(latitude))[:, None], (rows, lanes))
    turning = jnp.asarray(np.ascontiguousarray(turning, dtype=np.float32))
    results = pl.pallas_call(
        functools.partial(kernel, slices, cells),
        out_shape=(f32(*start_states.shape), f32(*start_states.shape), f32(share, lanes)),
        in_specs=[hbm] * 8,
        out_specs=(left, left, pl.BlockSpec(memory_space=pltpu.VMEM)),
        scratch_shapes=[
            f32(3, rows, lanes),
            pltpu.VMEM((rows, lanes), jnp.int32),
            pltpu.VMEM((rows, lanes), jnp.int32),
            pltpu.SMEM(class_depth.shape, jnp.float32),
            f32(rows, lanes),
            f32(2, rows, lanes),
            f32(5, 2, rows, lanes),
            f32(rows, lanes),
            f32(2 * STEPS, lanes),
            f32(2, rows, lanes),
            f32(STEPS + 1, 2, rows, lanes),
            f32(STEPS + 1, 2, rows, lanes),
            f32(2, rows, lanes),
            f32(2, wide, lanes),
            f32(2, wide, lanes),
            f32(2, rows + rim_rows, lanes),
            f32(2, rows + rim_rows, lanes),
            f32(rim_rows, lanes),
            f32(rim_rows, lanes),
            f32(3, rows, lanes),
            f32(3, rows, lanes),
            f32(3, rows, lanes),
            f32(3, rows, lanes),
            f32(2, rows, lanes),
            f32(slices, share, lanes),
            f32(slices, share, lanes),
            sems((8,)),
            sems((2,)),
            sems((2, math.gcd(slices, 8))),
            sems((2, math.gcd(slices, 8))),
            sems((2,)),
            sems((2,)),
            sems,
            sems,
            sems,
            sems,
            sems,
            sems,
            sems((slices,)),
            sems((slices,)),
        ],
        compiler_params=pltpu.CompilerParams(
            collective_id=0, has_side_effects=True, vmem_limit_bytes=32 * 1024 * 1024
        ),
    )(
        *(pltpu.with_memory_space_constraint(x, pltpu.HBM) for x in (*operands, turning)),
    )
    return pl.pallas_call(
        handed_over,
        out_shape=tuple(jax.ShapeDtypeStruct(r.shape, r.dtype) for r in results),
        in_specs=[left] * 3,
        out_specs=(hbm,) * 3,
        scratch_shapes=[sems((3,))],
        compiler_params=pltpu.CompilerParams(vmem_limit_bytes=16 * 1024 * 1024),
    )(*results)


def solution(mesh):
    return jax.shard_map(
        functools.partial(local, mesh.shape["tm"], mesh.shape["cell"]),
        mesh=mesh,
        in_specs=(
            P("tm", None, None, "cell"),
            P(None, "cell"),
            P(None, "cell"),
            P(),
            P(None, "cell"),
            P(None, "cell"),
            P(None, "cell"),
        ),
        out_specs=(P("tm", None, None, "cell"), P("tm", None, None, "cell"), P("tm", "cell")),
        check_vma=False,
    )
```
